512 devices in a mesh: ax: 32 (over x, y), tr: 16 (over z, core).
Axes of the slice: x: 4, y: 8, z: 8, core: 2. Of those that a mesh axis runs over, the one named last changes fastest.
Arguments:
- solid_old: float32 [512, 512, 512], P('ax', 'tr'), may hold values from -6 to 6
- gas_rate: bfloat16 [512, 512, 512], P('ax', 'tr'), may hold values from 0 to 1, as said below
- gas_inlet: float32 [512, 512], P('tr'), may hold values from -6 to 6
Outputs:
- gas_new: float32 [512, 512, 512], P('ax', 'tr')
- solid_new: float32 [512, 512, 512], P('ax', 'tr')
- temperature_gap: float32 [512, 512, 512], P('ax', 'tr')
The draws below stay inside these ranges and needn't reach their ends.
Inputs may be any that keep to these rules, and one draw needn't show every extreme that they name: `gas_rate`: positive transfer numbers.
All inputs are finite; a program needn't handle non-finite values.
Results may differ from the reference program's by a relative error of at most 0.0013.
Values sent between devices are 32-bit elements; how exact they have to be, the bound alone decides.
A program may use at most 64 MiB of HBM per device.

```python
import math
import jax
import jax.numpy as jnp
from jax import lax

NX = 512
NY = 512
AXIAL_PLANES = 512


def draw_gas_rate(key, part):
    key = jax.random.fold_in(key, 11)
    random_keys = jax.random.split(key, 4)
    slow_share = 0.5
    select = jax.random.uniform(random_keys[0], (NY, NX), jnp.float32)
    baseline_rate = jnp.where(select < slow_share, 1.0 / AXIAL_PLANES, 1.0 / 40.0)
    row_multiplier = jnp.exp(jax.random.uniform(random_keys[1], (NY, 1), jnp.float32, -0.35, 0.35))
    cell_multiplier = jnp.exp(jax.random.uniform(random_keys[2], (AXIAL_PLANES, NY, NX), jnp.float32, -0.5, 0.5))
    surge_planes = jax.random.randint(random_keys[3], (2,), 0, AXIAL_PLANES)
    plane_numbers = jnp.arange(AXIAL_PLANES, dtype=jnp.int32)
    surge_plane_count = jnp.sum((plane_numbers[:, None] == surge_planes[None, :]).astype(jnp.float32), axis=1)
    surge_rate = 0.3 * surge_plane_count[:, None, None]
    plane_rates = baseline_rate[None, :, :] * row_multiplier[None, :, :] * cell_multiplier + surge_rate
    return plane_rates.astype(jnp.bfloat16)


def levels(key, extent, shards, smallest, high):
    def one(axis_at, shards_of):
        steps = jax.random.uniform(jax.random.fold_in(jax.random.fold_in(key, 6), axis_at), (shards_of,), jnp.float32, smallest / len(shards), high / len(shards))
        return jnp.repeat(jnp.exp(steps), extent[axis_at] // shards_of).reshape((-1,) + (1,) * (len(extent) - axis_at - 1))

    factor_of = one(*shards[0])
    for cut in shards[1:]:
        factor_of = factor_of * one(*cut)
    return factor_of


def centred(own_key, shape, width, reach, pieces=(), held_as=jnp.bfloat16):
    array = width * jax.random.normal(own_key, shape, jnp.float32)
    if pieces:
        array = array * levels(own_key, shape, pieces, -0.22, 0.18)
    return jnp.clip(array, -reach, reach).astype(held_as)


def setup_inputs(seed: int = 0) -> dict:
    key_list = jax.random.split(jax.random.key(seed), 4)
    return {
        "solid_old": centred(key_list[0], (AXIAL_PLANES, NY, NX), 1.0, 6.0, ((0, 32), (1, 16)), jnp.float32),
        "gas_rate": draw_gas_rate(jax.random.fold_in(key_list[3], 71), 0),
        "gas_inlet": centred(key_list[2], (NY, NX), 1.0, 6.0, ((0, 16),), jnp.float32),
    }


COUPLE = 8.0
ALONG_ROW = 100.0
ACROSS_ROWS = 4000.0

def line_table(order_n, conduct):
    indices = jnp.arange(1, order_n + 1, dtype=jnp.int32)
    product = indices[:, None] * indices[None, :] % (2 * (order_n + 1))
    sine_table = jnp.sin(product.astype(jnp.float32) * (math.pi / (order_n + 1))) * math.sqrt(2.0 / (order_n + 1))
    wavenum = indices.astype(jnp.float32) * (math.pi / (order_n + 1))
    damping = 1.0 / (1.0 + conduct * (2.0 - 2.0 * jnp.cos(wavenum)))
    return jnp.dot(sine_table * damping[None, :], sine_table.T, precision=lax.Precision.HIGHEST)

def reference(solid_old, gas_rate, gas_inlet):
    plane_rates = gas_rate.astype(jnp.float32)

    def march(state, plane_pair):
        rate_plane, solid_plane = plane_pair
        new_state = (state + rate_plane * solid_plane) / (1.0 + rate_plane)
        return (new_state, new_state)
    last_plane, gas_new = lax.scan(march, gas_inlet.astype(jnp.float32), (plane_rates, solid_old))
    right_side = solid_old + COUPLE * plane_rates * (gas_new - solid_old)
    x_table = line_table(NX, ALONG_ROW)
    y_table = line_table(NY, ACROSS_ROWS)

    def solve_plane(plane_rhs):
        inner = jnp.dot(y_table, plane_rhs, precision=lax.Precision.HIGHEST)
        return jnp.dot(inner, x_table.T, precision=lax.Precision.HIGHEST)
    solid_new = lax.map(solve_plane, right_side)
    return (gas_new, solid_new, gas_new - solid_new)
```

```python
import functools
import math

import jax
import jax.numpy as jnp
import ml_dtypes
import numpy as np
from jax import lax
from jax.experimental import pallas as pl
from jax.experimental.pallas import tpu as pltpu
from jax.sharding import PartitionSpec as P

COUPLE = 8.0
ALONG_ROW = 100.0
ACROSS_ROWS = 4000.0
MESH = pl.DeviceIdType.MESH
F32 = jnp.float32
BF16 = jnp.bfloat16


def halves(table):
    high = table.astype(np.float32).astype(ml_dtypes.bfloat16)
    low = (table - high.astype(np.float64)).astype(np.float32).astype(ml_dtypes.bfloat16)
    return np.stack([high, low])


def line_inverse(order_n, conduct):
    theta = 2.0 * math.asinh(0.5 / math.sqrt(conduct))
    i = np.arange(1, order_n + 1, dtype=np.float64)
    near = np.minimum(i[:, None], i[None, :])
    far = order_n + 1 - np.maximum(i[:, None], i[None, :])
    return np.sinh(near * theta) * np.sinh(far * theta) / (
        conduct * math.sinh(theta) * math.sinh((order_n + 1) * theta)
    )


class Across:
    def __init__(self, rows, blocks, conduct, group):
        theta = 2.0 * math.asinh(0.5 / math.sqrt(conduct))
        self.kappa = 1.0 / (2.0 * conduct * math.sinh(theta))
        self.step = math.exp(-rows * theta)
        self.end = math.exp(-(rows * blocks + 1) * theta)
        self.reflect = -self.kappa * math.exp(-theta) / (1.0 - self.end**2)
        a = np.arange(1, rows + 1, dtype=np.float64)
        block = self.kappa * np.exp(-np.abs(a[:, None] - a[None, :]) * theta)
        self.local = halves(np.kron(np.eye(group), block))
        weights = np.stack(
            [
                np.exp(-(rows - a) * theta),
                np.exp(-(a - 1) * theta),
                np.exp(-a * theta),
                np.exp(-(rows + 1 - a) * theta),
            ]
        )
        self.weights = np.repeat(weights[:, :, None], 128, axis=2).astype(np.float32)


def dot3(a_high, a_low, b_high, b_low):
    dot = functools.partial(jnp.dot, preferred_element_type=F32)
    return dot(a_high, b_high) + (dot(a_low, b_high) + dot(a_high, b_low))


def split(value):
    high = value.astype(BF16)
    return high, (value - high.astype(F32)).astype(BF16)


def exchange_kernel(
    n_ax,
    n_tr,
    across,
    solid_hbm,
    rate_hbm,
    inlet_hbm,
    along_hbm,
    local_hbm,
    weights_hbm,
    gas_hbm,
    part_hbm,
    carry_out,
    solid,
    rate,
    inlet,
    along,
    local,
    weights,
    cumul,
    particular,
    gas,
    right_hi,
    right_lo,
    mid_hi,
    mid_lo,
    part,
    pieces,
    first,
    maps,
    flows,
    inflows,
    inflow,
    sums,
    sums_in,
    ends,
    ends_in,
    load_sem,
    store_sem,
    send_sem,
    recv_sem,
):
    me_ax = lax.axis_index("ax")
    me_tr = lax.axis_index("tr")
    planes, rows, cols = solid.shape
    col_tiles = cols // 128

    loads = [
        pltpu.make_async_copy(source, target, load_sem.at[i])
        for i, (source, target) in enumerate(
            [
                (rate_hbm, rate),
                (solid_hbm, solid),
                (inlet_hbm, inlet),
                (weights_hbm, weights),
                (local_hbm, local),
                (along_hbm, along),
            ]
        )
    ]
    for load in loads:
        load.start()

    barrier = pltpu.get_barrier_semaphore()

    def greet_ax(k, _):
        pl.semaphore_signal(
            barrier, inc=1, device_id=(lax.rem(me_ax + k, n_ax), me_tr), device_id_type=MESH
        )
        return 0

    def greet_tr(k, _):
        pl.semaphore_signal(
            barrier, inc=1, device_id=(me_ax, lax.rem(me_tr + k, n_tr)), device_id_type=MESH
        )
        return 0

    lax.fori_loop(1, n_ax, greet_ax, 0)
    lax.fori_loop(1, n_tr, greet_tr, 0)

    for load in loads[:3]:
        load.wait()

    upper = lax.broadcasted_iota(jnp.int32, (8, 128), 0) < 4

    def group_maps(g, _):
        at = pl.ds(pl.multiple_of(g * 16, 16), 16)

        def plane(p, state):
            factor, offset = state
            r = rate[p, at, :].astype(F32)
            keep = 1.0 / (1.0 + r)
            factor = factor * keep
            offset = offset * keep + r * solid[p, at, :] * keep
            cumul[p, at, :] = factor
            particular[p, at, :] = offset
            return factor, offset

        factor, offset = lax.fori_loop(
            0,
            planes,
            plane,
            (jnp.ones((16, cols), F32), jnp.zeros((16, cols), F32)),
            unroll=True,
        )
        start = inlet[at, :]
        for h in range(2):
            for c in range(col_tiles):
                box = (slice(8 * h, 8 * h + 8), slice(128 * c, 128 * c + 128))
                f, o, s = factor[box], offset[box], start[box]
                q = (g * 2 + h) * (2 * col_tiles) + 2 * c
                pieces[q] = jnp.where(upper, f, pltpu.roll(o, 4, 0))
                pieces[q + 1] = jnp.where(upper, pltpu.roll(f, 4, 0), o)
                first[q] = s
                first[q + 1] = pltpu.roll(s, 4, 0)
        return 0

    lax.fori_loop(0, rows // 16, group_maps, 0)

    pl.semaphore_wait(barrier, n_ax - 1 + n_tr - 1)

    def send_map(k, _):
        to = lax.rem(me_ax + k, n_ax)
        pltpu.make_async_remote_copy(
            src_ref=pieces.at[to],
            dst_ref=maps.at[me_ax],
            send_sem=send_sem.at[0],
            recv_sem=recv_sem.at[0],
            device_id=(to, me_tr),
            device_id_type=MESH,
        ).start()
        return 0

    lax.fori_loop(1, n_ax, send_map, 0)
    maps[me_ax] = pieces[me_ax]

    def wait_for(ref, count, sem):
        box = ref.at[pl.ds(0, count)]
        pltpu.make_async_copy(box, box, sem).wait()

    wait_for(maps, n_ax - 1, recv_sem.at[0])

    def march(k, state):
        flows[k] = state[:4]
        m = maps[k]
        return m * state + pltpu.roll(m, 4, 0)

    lax.fori_loop(0, n_ax, march, first[me_ax], unroll=True)

    def send_flow(k, _):
        to = lax.rem(me_ax + k, n_ax)
        pltpu.make_async_remote_copy(
            src_ref=flows.at[to],
            dst_ref=inflows.at[me_ax],
            send_sem=send_sem.at[1],
            recv_sem=recv_sem.at[1],
            device_id=(to, me_tr),
            device_id_type=MESH,
        ).start()
        return 0

    lax.fori_loop(1, n_ax, send_flow, 0)
    inflows[me_ax] = flows[me_ax]
    loads[3].wait()
    wait_for(inflows, n_ax - 1, recv_sem.at[1])

    for h in range(rows // 8):
        for c in range(col_tiles):
            q = h * 2 * col_tiles + 2 * c
            inflow[8 * h : 8 * h + 8, 128 * c : 128 * c + 128] = jnp.concatenate(
                [inflows[q], inflows[q + 1]], axis=0
            )

    def plane_group(g, _):
        for c in range(col_tiles):
            lanes = pl.ds(128 * c, 128)
            to_last, to_first = weights[0], weights[1]
            totals = []
            for j in range(4):
                p = g * 4 + j
                s = solid[p, :, lanes]
                r = rate[p, :, lanes].astype(F32)
                new = particular[p, :, lanes] + cumul[p, :, lanes] * inflow[:, lanes]
                gas[p, :, lanes] = new
                right = s + (COUPLE * r) * (new - s)
                at = pl.ds(pl.multiple_of(p * rows, rows), rows)
                right_hi[at, lanes], right_lo[at, lanes] = split(right)
                totals.append(
                    (
                        jnp.sum(right * to_last, axis=0, keepdims=True),
                        jnp.sum(right * to_first, axis=0, keepdims=True),
                    )
                )
            sums[g * col_tiles + c] = jnp.concatenate(
                [t[0] for t in totals] + [t[1] for t in totals], axis=0
            )
        return 0

    lax.fori_loop(0, planes // 4, plane_group, 0)

    def send_sum(k, _):
        to = lax.rem(me_tr + k, n_tr)
        pltpu.make_async_remote_copy(
            src_ref=sums.at[to],
            dst_ref=sums_in.at[me_tr],
            send_sem=send_sem.at[2],
            recv_sem=recv_sem.at[2],
            device_id=(me_ax, to),
            device_id_type=MESH,
        ).start()
        return 0

    lax.fori_loop(1, n_tr, send_sum, 0)
    sums_in[me_tr] = sums[me_tr]

    gas_copy = pltpu.make_async_copy(gas, gas_hbm, store_sem.at[0])
    gas_copy.start()

    loads[4].wait()
    group = local.shape[1]

    def local_solve(g, _):
        at = pl.ds(pl.multiple_of(g * group, group), group)
        mid = dot3(local[0], local[1], right_hi[at, :], right_lo[at, :])
        mid_hi[at, :], mid_lo[at, :] = split(mid)
        return 0

    lax.fori_loop(0, planes * rows // group, local_solve, 0)

    wait_for(sums_in, n_tr - 1, recv_sem.at[2])

    forward = [jnp.zeros((8, 128), F32)]
    for d in range(n_tr):
        forward.append(across.step * forward[-1] + sums_in[d])
    backward = [jnp.zeros((8, 128), F32)]
    for d in reversed(range(n_tr)):
        backward.append(across.step * backward[-1] + sums_in[d])
    whole = jnp.where(upper, forward[-1], backward[-1])
    mirror = across.reflect * (pltpu.roll(whole, 4, 0) - across.end * whole)
    for d in range(n_tr):
        inner = jnp.where(upper, forward[d], backward[n_tr - 1 - d])
        fade = jnp.where(upper, across.step**d, across.step ** (n_tr - 1 - d))
        ends[d] = across.kappa * inner + mirror * fade

    def ends_box(owner):
        return ends_in.at[
            pl.ds(pl.multiple_of(owner // col_tiles * 8, 8), 8),
            pl.ds(pl.multiple_of(lax.rem(owner, col_tiles) * 128, 128), 128),
        ]

    def send_end(k, _):
        to = lax.rem(me_tr + k, n_tr)
        pltpu.make_async_remote_copy(
            src_ref=ends.at[to],
            dst_ref=ends_box(me_tr),
            send_sem=send_sem.at[3],
            recv_sem=recv_sem.at[3],
            device_id=(me_ax, to),
            device_id_type=MESH,
        ).start()
        return 0

    lax.fori_loop(1, n_tr, send_end, 0)
    ends_box(me_tr)[...] = ends[me_tr]

    loads[5].wait()

    def along_solve(g, _):
        at = pl.ds(pl.multiple_of(g * group, group), group)
        part[at, :] = dot3(mid_hi[at, :], mid_lo[at, :], along[0], along[1])
        return 0

    lax.fori_loop(0, planes * rows // group, along_solve, 0)
    part_copy = pltpu.make_async_copy(part, part_hbm, store_sem.at[1])
    part_copy.start()

    wait_for(ends, n_tr - 1, recv_sem.at[3])
    end_hi, end_lo = split(ends_in[...])
    carry_out[...] = dot3(end_hi, end_lo, along[0], along[1])

    gas_copy.wait()
    part_copy.wait()
    wait_for(pieces, n_ax - 1, send_sem.at[0])
    wait_for(flows, n_ax - 1, send_sem.at[1])
    wait_for(sums, n_tr - 1, send_sem.at[2])
    wait_for(ends, n_tr - 1, send_sem.at[3])


def finish_kernel(gas_in, part, carry, weights, gas_out, solid_out, gap_out):
    rows = part.shape[1]
    cols = part.shape[2]
    lanes_of = cols // 128
    before = jnp.concatenate([weights[2]] * lanes_of, axis=1)
    after = jnp.concatenate([weights[3]] * lanes_of, axis=1)
    for j in range(4):
        new = gas_in[j]
        solid = part[j] + (
            before * jnp.broadcast_to(carry[j : j + 1, :], (rows, cols))
            + after * jnp.broadcast_to(carry[4 + j : 5 + j, :], (rows, cols))
        )
        gas_out[j] = new
        solid_out[j] = solid
        gap_out[j] = new - solid


def per_device(n_ax, n_tr, solid_old, gas_rate, gas_inlet):
    planes, rows, cols = solid_old.shape
    across = Across(rows, n_tr, ACROSS_ROWS, 8)
    along = halves(line_inverse(cols, ALONG_ROW).T)
    weights = jnp.asarray(across.weights)
    tiles = cols // 128
    anywhere = pl.BlockSpec(memory_space=pl.ANY)
    cells = planes * rows
    gas, part, carry = pl.pallas_call(
        functools.partial(exchange_kernel, n_ax, n_tr, across),
        out_shape=(
            jax.ShapeDtypeStruct((planes, rows, cols), F32),
            jax.ShapeDtypeStruct((cells, cols), F32),
            jax.ShapeDtypeStruct((planes // 4 * 8, cols), F32),
        ),
        in_specs=[anywhere] * 6,
        out_specs=(anywhere, anywhere, pl.BlockSpec(memory_space=pltpu.VMEM)),
        scratch_shapes=[
            pltpu.VMEM((planes, rows, cols), F32),
            pltpu.VMEM((planes, rows, cols), BF16),
            pltpu.VMEM((rows, cols), F32),
            pltpu.VMEM((2, cols, cols), BF16),
            pltpu.VMEM(across.local.shape, BF16),
            pltpu.VMEM((4, rows, 128), F32),
            pltpu.VMEM((planes, rows, cols), F32),
            pltpu.VMEM((planes, rows, cols), F32),
            pltpu.VMEM((planes, rows, cols), F32),
            pltpu.VMEM((cells, cols), BF16),
            pltpu.VMEM((cells, cols), BF16),
            pltpu.VMEM((cells, cols), BF16),
            pltpu.VMEM((cells, cols), BF16),
            pltpu.VMEM((cells, cols), F32),
            pltpu.VMEM((n_ax, 8, 128), F32),
            pltpu.VMEM((n_ax, 8, 128), F32),
            pltpu.VMEM((n_ax, 8, 128), F32),
            pltpu.VMEM((n_ax, 4, 128), F32),
            pltpu.VMEM((n_ax, 4, 128), F32),
            pltpu.VMEM((rows, cols), F32),
            pltpu.VMEM((n_tr, 8, 128), F32),
            pltpu.VMEM((n_tr, 8, 128), F32),
            pltpu.VMEM((n_tr, 8, 128), F32),
            pltpu.VMEM((planes // 4 * 8, cols), F32),
            pltpu.SemaphoreType.DMA((6,)),
            pltpu.SemaphoreType.DMA((2,)),
            pltpu.SemaphoreType.DMA((4,)),
            pltpu.SemaphoreType.DMA((4,)),
        ],
        compiler_params=pltpu.CompilerParams(
            collective_id=0, has_side_effects=True, vmem_limit_bytes=32 * 2**20
        ),
        name="exchange",
    )(solid_old, gas_rate, gas_inlet, jnp.asarray(along), jnp.asarray(across.local), weights)

    field = pl.BlockSpec((4, rows, cols), lambda g: (g, 0, 0))
    shape = jax.ShapeDtypeStruct((planes, rows, cols), F32)
    return pl.pallas_call(
        finish_kernel,
        grid=(planes // 4,),
        out_shape=(shape, shape, shape),
        in_specs=[
            field,
            field,
            pl.BlockSpec((8, cols), lambda g: (g, 0)),
            pl.BlockSpec((4, rows, 128), lambda g: (0, 0, 0)),
        ],
        out_specs=(field, field, field),
        compiler_params=pltpu.CompilerParams(vmem_limit_bytes=32 * 2**20),
        name="finish",
    )(gas, part.reshape(planes, rows, cols), carry, weights)


def solution(mesh):
    n_ax, n_tr = mesh.shape["ax"], mesh.shape["tr"]
    return jax.shard_map(
        functools.partial(per_device, n_ax, n_tr),
        mesh=mesh,
        in_specs=(P("ax", "tr", None), P("ax", "tr", None), P("tr", None)),
        out_specs=(P("ax", "tr", None), P("ax", "tr", None), P("ax", "tr", None)),
        check_vma=False,
    )
```

```python
import functools
import math

import jax
import jax.numpy as jnp
import ml_dtypes
import numpy as np
from jax import lax
from jax.experimental import pallas as pl
from jax.experimental.pallas import tpu as pltpu
from jax.sharding import PartitionSpec as P

COUPLE = 8.0
ALONG_ROW = 100.0
ACROSS_ROWS = 4000.0
MESH = pl.DeviceIdType.MESH
F32 = jnp.float32
BF16 = jnp.bfloat16


def halves(table):
    high = table.astype(np.float32).astype(ml_dtypes.bfloat16)
    low = (table - high.astype(np.float64)).astype(np.float32).astype(ml_dtypes.bfloat16)
    return np.stack([high, low])


def line_inverse(order_n, conduct):
    theta = 2.0 * math.asinh(0.5 / math.sqrt(conduct))
    i = np.arange(1, order_n + 1, dtype=np.float64)
    near = np.minimum(i[:, None], i[None, :])
    far = order_n + 1 - np.maximum(i[:, None], i[None, :])
    return np.sinh(near * theta) * np.sinh(far * theta) / (
        conduct * math.sinh(theta) * math.sinh((order_n + 1) * theta)
    )


class Across:
    def __init__(self, rows, blocks, conduct, group):
        theta = 2.0 * math.asinh(0.5 / math.sqrt(conduct))
        self.kappa = 1.0 / (2.0 * conduct * math.sinh(theta))
        self.step = math.exp(-rows * theta)
        self.end = math.exp(-(rows * blocks + 1) * theta)
        self.reflect = -self.kappa * math.exp(-theta) / (1.0 - self.end**2)
        a = np.arange(1, rows + 1, dtype=np.float64)
        block = self.kappa * np.exp(-np.abs(a[:, None] - a[None, :]) * theta)
        self.local = halves(np.kron(np.eye(group), block))
        self.theta = theta

    def fade_down(self, rows, first):
        row = lax.broadcasted_iota(jnp.int32, (rows, 128), 0)
        return jnp.exp((row + first).astype(F32) * -self.theta)

    def fade_up(self, rows, last):
        row = lax.broadcasted_iota(jnp.int32, (rows, 128), 0)
        return jnp.exp((rows - 1 + last - row).astype(F32) * -self.theta)


def dot3(a_high, a_low, b_high, b_low):
    dot = functools.partial(jnp.dot, preferred_element_type=F32)
    return dot(a_high, b_high) + (dot(a_low, b_high) + dot(a_high, b_low))


def split(value):
    high = value.astype(BF16)
    return high, (value - high.astype(F32)).astype(BF16)


def exchange_kernel(
    n_ax,
    n_tr,
    across,
    solid_hbm,
    rate_hbm,
    inlet_hbm,
    along_hbm,
    local_hbm,
    gas,
    part,
    carry,
    solid,
    rate,
    inlet,
    along,
    local,
    cumul,
    particular,
    right_hi,
    right_lo,
    mid_hi,
    mid_lo,
    pieces,
    first,
    maps,
    flows,
    inflows,
    inflow,
    sums,
    sums_in,
    ends,
    ends_in,
    load_sem,
    send_sem,
    recv_sem,
):
    me_ax = lax.axis_index("ax")
    me_tr = lax.axis_index("tr")
    planes, rows, cols = solid.shape
    col_tiles = cols // 128

    loads = [
        pltpu.make_async_copy(source, target, load_sem.at[i])
        for i, (source, target) in enumerate(
            [
                (rate_hbm, rate),
                (solid_hbm, solid),
                (inlet_hbm, inlet),
                (local_hbm, local),
                (along_hbm, along),
            ]
        )
    ]
    for load in loads:
        load.start()

    barrier = pltpu.get_barrier_semaphore()

    def greet_ax(k, _):
        pl.semaphore_signal(
            barrier, inc=1, device_id=(lax.rem(me_ax + k, n_ax), me_tr), device_id_type=MESH
        )
        return 0

    def greet_tr(k, _):
        pl.semaphore_signal(
            barrier, inc=1, device_id=(me_ax, lax.rem(me_tr + k, n_tr)), device_id_type=MESH
        )
        return 0

    lax.fori_loop(1, n_ax, greet_ax, 0)
    lax.fori_loop(1, n_tr, greet_tr, 0)

    for load in loads[:3]:
        load.wait()

    upper = lax.broadcasted_iota(jnp.int32, (8, 128), 0) < 4

    def group_maps(g, _):
        at = pl.ds(pl.multiple_of(g * 16, 16), 16)

        def plane(p, state):
            factor, offset = state
            r = rate[p, at, :].astype(F32)
            keep = 1.0 / (1.0 + r)
            factor = factor * keep
            offset = offset * keep + r * solid[p, at, :] * keep
            cumul[p, at, :] = factor
            particular[p, at, :] = offset
            return factor, offset

        factor, offset = lax.fori_loop(
            0,
            planes,
            plane,
            (jnp.ones((16, cols), F32), jnp.zeros((16, cols), F32)),
            unroll=True,
        )
        start = inlet[at, :]
        for h in range(2):
            for c in range(col_tiles):
                box = (slice(8 * h, 8 * h + 8), slice(128 * c, 128 * c + 128))
                f, o, s = factor[box], offset[box], start[box]
                q = (g * 2 + h) * (2 * col_tiles) + 2 * c
                pieces[q] = jnp.where(upper, f, pltpu.roll(o, 4, 0))
                pieces[q + 1] = jnp.where(upper, pltpu.roll(f, 4, 0), o)
                first[q] = s
                first[q + 1] = pltpu.roll(s, 4, 0)
        return 0

    lax.fori_loop(0, rows // 16, group_maps, 0)

    pl.semaphore_wait(barrier, n_ax - 1 + n_tr - 1)

    def send_map(k, _):
        to = lax.rem(me_ax + k, n_ax)
        pltpu.make_async_remote_copy(
            src_ref=pieces.at[to],
            dst_ref=maps.at[me_ax],
            send_sem=send_sem.at[0],
            recv_sem=recv_sem.at[0],
            device_id=(to, me_tr),
            device_id_type=MESH,
        ).start()
        return 0

    lax.fori_loop(1, n_ax, send_map, 0)
    maps[me_ax] = pieces[me_ax]

    def wait_for(ref, count, sem):
        box = ref.at[pl.ds(0, count)]
        pltpu.make_async_copy(box, box, sem).wait()

    wait_for(maps, n_ax - 1, recv_sem.at[0])

    def march(k, state):
        flows[k] = state[:4]
        m = maps[k]
        return m * state + pltpu.roll(m, 4, 0)

    lax.fori_loop(0, n_ax, march, first[me_ax], unroll=True)

    def send_flow(k, _):
        to = lax.rem(me_ax + k, n_ax)
        pltpu.make_async_remote_copy(
            src_ref=flows.at[to],
            dst_ref=inflows.at[me_ax],
            send_sem=send_sem.at[1],
            recv_sem=recv_sem.at[1],
            device_id=(to, me_tr),
            device_id_type=MESH,
        ).start()
        return 0

    lax.fori_loop(1, n_ax, send_flow, 0)
    inflows[me_ax] = flows[me_ax]
    wait_for(inflows, n_ax - 1, recv_sem.at[1])

    for h in range(rows // 8):
        for c in range(col_tiles):
            q = h * 2 * col_tiles + 2 * c
            inflow[8 * h : 8 * h + 8, 128 * c : 128 * c + 128] = jnp.concatenate(
                [inflows[q], inflows[q + 1]], axis=0
            )

    to_last, to_first = across.fade_up(rows, 0), across.fade_down(rows, 0)

    def plane_group(g, _):
        for c in range(col_tiles):
            lanes = pl.ds(128 * c, 128)
            totals = []
            for j in range(4):
                p = g * 4 + j
                s = solid[p, :, lanes]
                r = rate[p, :, lanes].astype(F32)
                new = particular[p, :, lanes] + cumul[p, :, lanes] * inflow[:, lanes]
                gas[p, :, lanes] = new
                right = s + (COUPLE * r) * (new - s)
                at = pl.ds(pl.multiple_of(p * rows, rows), rows)
                right_hi[at, lanes], right_lo[at, lanes] = split(right)
                totals.append(
                    (
                        jnp.sum(right * to_last, axis=0, keepdims=True),
                        jnp.sum(right * to_first, axis=0, keepdims=True),
                    )
                )
            sums[g * col_tiles + c] = jnp.concatenate(
                [t[0] for t in totals] + [t[1] for t in totals], axis=0
            )
        return 0

    lax.fori_loop(0, planes // 4, plane_group, 0)

    def send_sum(k, _):
        to = lax.rem(me_tr + k, n_tr)
        pltpu.make_async_remote_copy(
            src_ref=sums.at[to],
            dst_ref=sums_in.at[me_tr],
            send_sem=send_sem.at[2],
            recv_sem=recv_sem.at[2],
            device_id=(me_ax, to),
            device_id_type=MESH,
        ).start()
        return 0

    lax.fori_loop(1, n_tr, send_sum, 0)
    sums_in[me_tr] = sums[me_tr]

    loads[3].wait()
    group = local.shape[1]

    def local_solve(g, _):
        at = pl.ds(pl.multiple_of(g * group, group), group)
        mid = dot3(local[0], local[1], right_hi[at, :], right_lo[at, :])
        mid_hi[at, :], mid_lo[at, :] = split(mid)
        return 0

    lax.fori_loop(0, planes * rows // group, local_solve, 0)

    wait_for(sums_in, n_tr - 1, recv_sem.at[2])

    forward = [jnp.zeros((8, 128), F32)]
    for d in range(n_tr):
        forward.append(across.step * forward[-1] + sums_in[d])
    backward = [jnp.zeros((8, 128), F32)]
    for d in reversed(range(n_tr)):
        backward.append(across.step * backward[-1] + sums_in[d])
    whole = jnp.where(upper, forward[-1], backward[-1])
    mirror = across.reflect * (pltpu.roll(whole, 4, 0) - across.end * whole)
    for d in range(n_tr):
        inner = jnp.where(upper, forward[d], backward[n_tr - 1 - d])
        fade = jnp.where(upper, across.step**d, across.step ** (n_tr - 1 - d))
        ends[d] = across.kappa * inner + mirror * fade

    def ends_box(owner):
        return ends_in.at[
            pl.ds(pl.multiple_of(owner // col_tiles * 8, 8), 8),
            pl.ds(pl.multiple_of(lax.rem(owner, col_tiles) * 128, 128), 128),
        ]

    def send_end(k, _):
        to = lax.rem(me_tr + k, n_tr)
        pltpu.make_async_remote_copy(
            src_ref=ends.at[to],
            dst_ref=ends_box(me_tr),
            send_sem=send_sem.at[3],
            recv_sem=recv_sem.at[3],
            device_id=(me_ax, to),
            device_id_type=MESH,
        ).start()
        return 0

    lax.fori_loop(1, n_tr, send_end, 0)
    ends_box(me_tr)[...] = ends[me_tr]

    loads[4].wait()

    def along_solve(g, _):
        at = pl.ds(pl.multiple_of(g * group, group), group)
        part[at, :] = dot3(mid_hi[at, :], mid_lo[at, :], along[0], along[1])
        return 0

    lax.fori_loop(0, planes * rows // group, along_solve, 0)

    wait_for(ends, n_tr - 1, recv_sem.at[3])
    end_hi, end_lo = split(ends_in[...])
    carry[...] = dot3(end_hi, end_lo, along[0], along[1])

    wait_for(pieces, n_ax - 1, send_sem.at[0])
    wait_for(flows, n_ax - 1, send_sem.at[1])
    wait_for(sums, n_tr - 1, send_sem.at[2])
    wait_for(ends, n_tr - 1, send_sem.at[3])


def finish_kernel(across, gas_in, part, carry, gas_out, solid_out, gap_out):
    rows = part.shape[1]
    cols = part.shape[2]
    lanes_of = cols // 128
    before = jnp.concatenate([across.fade_down(rows, 1)] * lanes_of, axis=1)
    after = jnp.concatenate([across.fade_up(rows, 1)] * lanes_of, axis=1)
    for j in range(4):
        new = gas_in[j]
        solid = part[j] + (
            before * jnp.broadcast_to(carry[j : j + 1, :], (rows, cols))
            + after * jnp.broadcast_to(carry[4 + j : 5 + j, :], (rows, cols))
        )
        gas_out[j] = new
        solid_out[j] = solid
        gap_out[j] = new - solid


def far(value):
    return pltpu.with_memory_space_constraint(value, pltpu.HBM)


def per_device(n_ax, n_tr, solid_old, gas_rate, gas_inlet):
    planes, rows, cols = solid_old.shape
    across = Across(rows, n_tr, ACROSS_ROWS, 8)
    along = halves(line_inverse(cols, ALONG_ROW).T)
    tiles = cols // 128
    anywhere = pl.BlockSpec(memory_space=pl.ANY)
    cells = planes * rows
    gas, part, carry = pl.pallas_call(
        functools.partial(exchange_kernel, n_ax, n_tr, across),
        out_shape=(
            pltpu.VMEM((planes, rows, cols), F32),
            pltpu.VMEM((cells, cols), F32),
            pltpu.VMEM((planes // 4 * 8, cols), F32),
        ),
        in_specs=[anywhere] * 5,
        out_specs=[pl.BlockSpec(memory_space=pltpu.VMEM)] * 3,
        scratch_shapes=[
            pltpu.VMEM((planes, rows, cols), F32),
            pltpu.VMEM((planes, rows, cols), BF16),
            pltpu.VMEM((rows, cols), F32),
            pltpu.VMEM((2, cols, cols), BF16),
            pltpu.VMEM(across.local.shape, BF16),
            pltpu.VMEM((planes, rows, cols), F32),
            pltpu.VMEM((planes, rows, cols), F32),
            pltpu.VMEM((cells, cols), BF16),
            pltpu.VMEM((cells, cols), BF16),
            pltpu.VMEM((cells, cols), BF16),
            pltpu.VMEM((cells, cols), BF16),
            pltpu.VMEM((n_ax, 8, 128), F32),
            pltpu.VMEM((n_ax, 8, 128), F32),
            pltpu.VMEM((n_ax, 8, 128), F32),
            pltpu.VMEM((n_ax, 4, 128), F32),
            pltpu.VMEM((n_ax, 4, 128), F32),
            pltpu.VMEM((rows, cols), F32),
            pltpu.VMEM((n_tr, 8, 128), F32),
            pltpu.VMEM((n_tr, 8, 128), F32),
            pltpu.VMEM((n_tr, 8, 128), F32),
            pltpu.VMEM((planes // 4 * 8, cols), F32),
            pltpu.SemaphoreType.DMA((5,)),
            pltpu.SemaphoreType.DMA((4,)),
            pltpu.SemaphoreType.DMA((4,)),
        ],
        compiler_params=pltpu.CompilerParams(
            collective_id=0, has_side_effects=True, vmem_limit_bytes=32 * 2**20
        ),
        name="exchange",
    )(*map(far, (solid_old, gas_rate, gas_inlet, jnp.asarray(along), jnp.asarray(across.local))))

    field = pl.BlockSpec((4, rows, cols), lambda g: (g, 0, 0))
    shape = jax.ShapeDtypeStruct((planes, rows, cols), F32)
    return pl.pallas_call(
        functools.partial(finish_kernel, across),
        grid=(planes // 4,),
        out_shape=(shape, shape, shape),
        in_specs=[
            field,
            field,
            pl.BlockSpec((8, cols), lambda g: (g, 0)),
        ],
        out_specs=(field, field, field),
        compiler_params=pltpu.CompilerParams(vmem_limit_bytes=32 * 2**20),
        name="finish",
    )(gas, part.reshape(planes, rows, cols), carry)


def solution(mesh):
    n_ax, n_tr = mesh.shape["ax"], mesh.shape["tr"]
    return jax.shard_map(
        functools.partial(per_device, n_ax, n_tr),
        mesh=mesh,
        in_specs=(P("ax", "tr", None), P("ax", "tr", None), P("tr", None)),
        out_specs=(P("ax", "tr", None), P("ax", "tr", None), P("ax", "tr", None)),
        check_vma=False,
    )
```

```python
import functools
import math

import jax
import jax.numpy as jnp
import ml_dtypes
import numpy as np
from jax import lax
from jax.experimental import pallas as pl
from jax.experimental.pallas import tpu as pltpu
from jax.sharding import PartitionSpec as P

COUPLE = 8.0
ALONG_ROW = 100.0
ACROSS_ROWS = 4000.0
MESH = pl.DeviceIdType.MESH
F32 = jnp.float32
BF16 = jnp.bfloat16


def halves(table):
    high = table.astype(np.float32).astype(ml_dtypes.bfloat16)
    low = (table - high.astype(np.float64)).astype(np.float32).astype(ml_dtypes.bfloat16)
    return np.stack([high, low])


def line_inverse(order_n, conduct):
    theta = 2.0 * math.asinh(0.5 / math.sqrt(conduct))
    i = np.arange(1, order_n + 1, dtype=np.float64)
    near = np.minimum(i[:, None], i[None, :])
    far = order_n + 1 - np.maximum(i[:, None], i[None, :])
    return np.sinh(near * theta) * np.sinh(far * theta) / (
        conduct * math.sinh(theta) * math.sinh((order_n + 1) * theta)
    )


class Across:
    def __init__(self, rows, blocks, conduct, group):
        self.rows = rows
        self.last = rows * blocks + 1
        self.theta = 2.0 * math.asinh(0.5 / math.sqrt(conduct))
        kappa = 1.0 / (2.0 * conduct * math.sinh(self.theta))
        a = np.arange(1, rows + 1, dtype=np.float64)
        block = kappa * np.exp(-np.abs(a[:, None] - a[None, :]) * self.theta)
        self.local = halves(np.kron(np.eye(group), block))
        self.pair = 0.5 / (conduct * math.sinh(self.theta) * math.sinh(self.last * self.theta))
        end = math.exp(-self.last * self.theta)
        self.near = -kappa / (1.0 - end**2)
        self.cross = kappa * end / (1.0 - end**2) * math.exp(-(self.last - rows) * self.theta)

    def fade_down(self, first):
        row = lax.broadcasted_iota(jnp.int32, (self.rows, 128), 0)
        return jnp.exp((row + first).astype(F32) * -self.theta)

    def fade_up(self, last):
        row = lax.broadcasted_iota(jnp.int32, (self.rows, 128), 0)
        return jnp.exp((self.rows - 1 + last - row).astype(F32) * -self.theta)

    def power(self, steps, lanes):
        return jnp.exp(jnp.full((8, lanes), steps, jnp.int32).astype(F32) * self.theta)

    def sums(self, block, to_last, to_first):
        rows, lanes = self.rows, to_last.shape[1]
        power = functools.partial(self.power, lanes=lanes)
        before = rows * block
        return (
            0.5 * (power(before + rows) * to_last - power(-before - 1) * to_first),
            0.5
            * (
                power(self.last - before - 1) * to_first
                - power(before + rows - self.last) * to_last
            ),
        )

    def fields(self, block, below, above, to_last, to_first):
        rows, lanes = self.rows, to_last.shape[1]
        power = functools.partial(self.power, lanes=lanes)
        before = rows * block
        return (
            self.pair * (power(self.last - before) * below - power(-before) * above)
            + self.cross * to_last
            + self.near * power(-2 * before - 1) * to_first,
            self.pair
            * (power(before + rows + 1) * above - power(before + rows + 1 - self.last) * below)
            + self.cross * to_first
            + self.near * power(2 * before + 2 * rows + 1 - 2 * self.last) * to_last,
        )


def dot3(a_high, a_low, b_high, b_low):
    dot = functools.partial(jnp.dot, preferred_element_type=F32)
    return dot(a_high, b_high) + (dot(a_low, b_high) + dot(a_high, b_low))


def split(value):
    high = value.astype(BF16)
    return high, (value - high.astype(F32)).astype(BF16)


def exchange_kernel(
    n_ax,
    n_tr,
    across,
    solid_hbm,
    rate_hbm,
    inlet_hbm,
    along_hbm,
    local_hbm,
    gas,
    part,
    carry,
    solid,
    rate,
    inlet,
    along,
    local,
    cumul,
    particular,
    right_hi,
    right_lo,
    mid_hi,
    mid_lo,
    pieces,
    maps,
    flows,
    inflow,
    own,
    sums,
    sums_in,
    twin_out,
    pairs,
    load_sem,
    send_sem,
    recv_sem,
):
    me_ax = lax.axis_index("ax")
    me_tr = lax.axis_index("tr")
    planes, rows, cols = solid.shape
    col_tiles = cols // 128
    half = planes // 2
    n_owner = pieces.shape[0]
    is_owner = me_ax < n_owner
    my_piece = jnp.where(is_owner, me_ax, 0)
    core = lax.rem(me_tr, 2)
    twin = me_tr + 1 - 2 * core

    first_rows, last_rows = pl.ds(0, rows // 2), pl.ds(rows // 2, rows // 2)
    loads = [
        pltpu.make_async_copy(source, target, load_sem.at[i])
        for i, (source, target) in enumerate(
            [
                (rate_hbm.at[:, first_rows], rate.at[:, first_rows]),
                (solid_hbm.at[:, first_rows], solid.at[:, first_rows]),
                (rate_hbm.at[:, last_rows], rate.at[:, last_rows]),
                (solid_hbm.at[:, last_rows], solid.at[:, last_rows]),
                (inlet_hbm, inlet),
                (local_hbm, local),
                (along_hbm, along),
            ]
        )
    ]
    for load in loads[:5]:
        load.start()

    barrier = pltpu.get_barrier_semaphore()

    def greet(ax, tr):
        pl.semaphore_signal(barrier, inc=1, device_id=(ax, tr), device_id_type=MESH)

    @pl.when(is_owner)
    def _():
        def one(k, _):
            greet(lax.rem(me_ax + k, n_ax), me_tr)
            return 0

        lax.fori_loop(1, n_ax, one, 0)

    def greet_tr(k, _):
        greet(me_ax, lax.rem(me_tr + k, n_tr))
        return 0

    lax.fori_loop(1, n_tr, greet_tr, 0)

    for g in range(2):
        loads[2 * g].wait()
        loads[2 * g + 1].wait()
        if g == 1:
            loads[4].wait()
            loads[5].start()
            loads[6].start()
        at = pl.ds(g * 16, 16)

        def plane(p, state, at=at):
            factor, offset = state
            r = rate[p, at, :].astype(F32)
            near_keep = pl.reciprocal(1.0 + r, approx=True)
            keep = near_keep * (2.0 - (1.0 + r) * near_keep)
            factor = factor * keep
            offset = (offset + r * solid[p, at, :]) * keep
            cumul[p, at, :] = factor
            particular[p, at, :] = offset
            return factor, offset

        factor, offset = lax.fori_loop(
            0,
            planes,
            plane,
            (jnp.ones((16, cols), F32), jnp.zeros((16, cols), F32)),
            unroll=True,
        )
        for h in range(2):
            for c in range(col_tiles):
                box = (slice(8 * h, 8 * h + 8), slice(128 * c, 128 * c + 128))
                q = (g * 2 + h) * col_tiles + c
                pieces[q, 0] = factor[box]
                pieces[q, 1] = offset[box]

    pl.semaphore_wait(barrier, jnp.where(is_owner, n_owner - 1, n_owner) + n_tr - 1)

    def send_map(k, _):
        to = lax.rem(me_ax + k, n_owner)

        @pl.when(to != me_ax)
        def _():
            pltpu.make_async_remote_copy(
                src_ref=pieces.at[to],
                dst_ref=maps.at[me_ax],
                send_sem=send_sem.at[0],
                recv_sem=recv_sem.at[0],
                device_id=(to, me_tr),
                device_id_type=MESH,
            ).start()

        return 0

    lax.fori_loop(0, n_owner, send_map, 0)

    def wait_for(ref, count, sem):
        box = ref.at[pl.ds(0, count)]
        pltpu.make_async_copy(box, box, sem).wait()

    def tile_of(ref, piece):
        return ref.at[
            pl.ds(pl.multiple_of(piece // col_tiles * 8, 8), 8),
            pl.ds(pl.multiple_of(lax.rem(piece, col_tiles) * 128, 128), 128),
        ]

    @pl.when(is_owner)
    def _():
        maps[me_ax] = pieces[my_piece]
        wait_for(maps, n_ax - 1, recv_sem.at[0])

        def march(k, state):
            flows[k] = state
            return maps[k, 0] * state + maps[k, 1]

        lax.fori_loop(0, n_ax, march, tile_of(inlet, my_piece)[...], unroll=True)

        def send_flow(k, _):
            to = lax.rem(k, 4) * 8 + k // 4

            @pl.when(to != me_ax)
            def _():
                pltpu.make_async_remote_copy(
                    src_ref=flows.at[to],
                    dst_ref=tile_of(inflow, my_piece),
                    send_sem=send_sem.at[1],
                    recv_sem=recv_sem.at[1],
                    device_id=(to, me_tr),
                    device_id_type=MESH,
                ).start()

            return 0

        lax.fori_loop(0, n_ax, send_flow, 0)
        tile_of(inflow, my_piece)[...] = flows[me_ax]
        wait_for(flows, n_owner - 1, recv_sem.at[1])

    @pl.when(jnp.logical_not(is_owner))
    def _():
        wait_for(flows, n_owner, recv_sem.at[1])

    def send_sum(to):
        pltpu.make_async_remote_copy(
            src_ref=sums.at[lax.rem(to, 2), (to < me_tr).astype(jnp.int32)],
            dst_ref=sums_in.at[me_tr],
            send_sem=send_sem.at[2],
            recv_sem=recv_sem.at[2],
            device_id=(me_ax, to),
            device_id_type=MESH,
        ).start()

    def plane_group(g, _):
        to_last, to_first = across.fade_up(0), across.fade_down(0)
        for c in range(col_tiles):
            lanes = pl.ds(128 * c, 128)
            totals = []
            for j in range(half):
                p = g * half + j
                s = solid[p, :, lanes]
                r = rate[p, :, lanes].astype(F32)
                new = particular[p, :, lanes] + cumul[p, :, lanes] * inflow[:, lanes]
                gas[p, :, lanes] = new
                right = s + (COUPLE * r) * (new - s)
                at = pl.ds(pl.multiple_of(p * rows, rows), rows)
                right_hi[at, lanes], right_lo[at, lanes] = split(right)
                totals.append(
                    (
                        jnp.sum(right * to_last, axis=0, keepdims=True),
                        jnp.sum(right * to_first, axis=0, keepdims=True),
                    )
                )
            last = jnp.concatenate([t[0] for t in totals], axis=0)
            start = jnp.concatenate([t[1] for t in totals], axis=0)
            own[g, 0, :, lanes], own[g, 1, :, lanes] = last, start
            sums[g, 0, :, lanes], sums[g, 1, :, lanes] = across.sums(me_tr, last, start)

        def send(k, _):
            to = 2 * k + g

            @pl.when(to != me_tr)
            def _():
                send_sum(to)

            return 0

        lax.fori_loop(0, n_tr // 2, send, 0)
        return 0

    lax.fori_loop(0, 2, plane_group, 0)
    sums_in[me_tr] = sums[core, core]

    loads[5].wait()
    loads[6].wait()
    group = local.shape[1]

    def own_solve(g, _):
        at = pl.ds(pl.multiple_of(g * group, group), group)
        mid = dot3(local[0], local[1], right_hi[at, :], right_lo[at, :])
        mid_hi[at, :], mid_lo[at, :] = split(mid)
        part[at, :] = dot3(mid_hi[at, :], mid_lo[at, :], along[0], along[1])
        return 0

    lax.fori_loop(0, planes * rows // group, own_solve, 0)

    wait_for(sums_in, n_tr - 1, recv_sem.at[2])

    nothing = jnp.zeros((half, cols), F32)

    def add(k, totals):
        value = sums_in[k]
        return tuple(
            total + jnp.where(test, value, 0.0)
            for total, test in zip(totals, (k < me_tr, k > me_tr, k < twin, k > twin))
        )

    mine = lax.fori_loop(0, n_tr, add, (nothing,) * 4, unroll=True)
    twin_out[0], twin_out[1] = mine[2], mine[3]
    to_twin = pltpu.make_async_remote_copy(
        src_ref=twin_out,
        dst_ref=pairs.at[core],
        send_sem=send_sem.at[3],
        recv_sem=recv_sem.at[3],
        device_id=(me_ax, twin),
        device_id_type=MESH,
    )
    to_twin.start()
    pairs[core, 0], pairs[core, 1] = mine[0], mine[1]

    to_twin.wait_recv()
    fields = []
    for g in range(2):
        fields.extend(
            across.fields(me_tr, pairs[g, 0], pairs[g, 1], own[g, 0], own[g, 1])
        )
    end_hi, end_lo = split(jnp.concatenate(fields, axis=0))
    carry[...] = dot3(end_hi, end_lo, along[0], along[1])

    to_twin.wait_send()
    wait_for(sums_in, n_tr - 1, send_sem.at[2])

    @pl.when(is_owner)
    def _():
        wait_for(pieces, n_owner - 1, send_sem.at[0])
        wait_for(flows, n_ax - 1, send_sem.at[1])

    @pl.when(jnp.logical_not(is_owner))
    def _():
        wait_for(pieces, n_owner, send_sem.at[0])


def finish_kernel(across, gas, part, carry, gas_hbm, solid_hbm, gap_hbm, solid, gap, store_sem):
    planes, rows, cols = gas.shape
    half = planes // 2
    gas_store = pltpu.make_async_copy(gas, gas_hbm, store_sem.at[0, 0])
    gas_store.start()
    before = jnp.concatenate([across.fade_down(1)] * (cols // 128), axis=1)
    after = jnp.concatenate([across.fade_up(1)] * (cols // 128), axis=1)
    stores = []
    for p in range(planes):
        row = p // half * planes + p % half
        new = part[p] + (
            before * jnp.broadcast_to(carry[row : row + 1, :], (rows, cols))
            + after * jnp.broadcast_to(carry[row + half : row + half + 1, :], (rows, cols))
        )
        solid[p] = new
        gap[p] = gas[p] - new
        if p % 2 == 1:
            for i, (source, target) in enumerate(((solid, solid_hbm), (gap, gap_hbm))):
                box = pl.ds(p - 1, 2)
                stores.append(
                    pltpu.make_async_copy(
                        source.at[box], target.at[box], store_sem.at[1 + i, p // 2]
                    )
                )
                stores[-1].start()
    gas_store.wait()
    for store in stores:
        store.wait()


def far(value):
    return pltpu.with_memory_space_constraint(value, pltpu.HBM)


def per_device(n_ax, n_tr, solid_old, gas_rate, gas_inlet):
    planes, rows, cols = solid_old.shape
    across = Across(rows, n_tr, ACROSS_ROWS, 8)
    along = halves(line_inverse(cols, ALONG_ROW).T)
    cells = planes * rows
    half = planes // 2
    pieces = (rows // 8) * (cols // 128)
    field = (planes, rows, cols)
    anywhere = pl.BlockSpec(memory_space=pl.ANY)
    near = pl.BlockSpec(memory_space=pltpu.VMEM)
    gas, part, carry = pl.pallas_call(
        functools.partial(exchange_kernel, n_ax, n_tr, across),
        out_shape=(
            pltpu.VMEM(field, F32),
            pltpu.VMEM((cells, cols), F32),
            pltpu.VMEM((2 * planes, cols), F32),
        ),
        in_specs=[anywhere] * 5,
        out_specs=[near] * 3,
        scratch_shapes=[
            pltpu.VMEM(field, F32),
            pltpu.VMEM(field, BF16),
            pltpu.VMEM((rows, cols), F32),
            pltpu.VMEM((2, cols, cols), BF16),
            pltpu.VMEM(across.local.shape, BF16),
            pltpu.VMEM(field, F32),
            pltpu.VMEM(field, F32),
            pltpu.VMEM((cells, cols), BF16),
            pltpu.VMEM((cells, cols), BF16),
            pltpu.VMEM((cells, cols), BF16),
            pltpu.VMEM((cells, cols), BF16),
            pltpu.VMEM((pieces, 2, 8, 128), F32),
            pltpu.VMEM((n_ax, 2, 8, 128), F32),
            pltpu.VMEM((n_ax, 8, 128), F32),
            pltpu.VMEM((rows, cols), F32),
            pltpu.VMEM((2, 2, half, cols), F32),
            pltpu.VMEM((2, 2, half, cols), F32),
            pltpu.VMEM((n_tr, half, cols), F32),
            pltpu.VMEM((2, half, cols), F32),
            pltpu.VMEM((2, 2, half, cols), F32),
            pltpu.SemaphoreType.DMA((7,)),
            pltpu.SemaphoreType.DMA((4,)),
            pltpu.SemaphoreType.DMA((4,)),
        ],
        compiler_params=pltpu.CompilerParams(
            collective_id=0, has_side_effects=True, vmem_limit_bytes=32 * 2**20
        ),
        name="exchange",
    )(*map(far, (solid_old, gas_rate, gas_inlet, jnp.asarray(along), jnp.asarray(across.local))))

    shape = jax.ShapeDtypeStruct(field, F32)
    return pl.pallas_call(
        functools.partial(finish_kernel, across),
        out_shape=(shape, shape, shape),
        in_specs=[near] * 3,
        out_specs=[anywhere] * 3,
        scratch_shapes=[
            pltpu.VMEM(field, F32),
            pltpu.VMEM(field, F32),
            pltpu.SemaphoreType.DMA((3, planes // 2)),
        ],
        compiler_params=pltpu.CompilerParams(vmem_limit_bytes=16 * 2**20),
        name="finish",
    )(gas, part.reshape(field), carry)


def solution(mesh):
    n_ax, n_tr = mesh.shape["ax"], mesh.shape["tr"]
    return jax.shard_map(
        functools.partial(per_device, n_ax, n_tr),
        mesh=mesh,
        in_specs=(P("ax", "tr", None), P("ax", "tr", None), P("tr", None)),
        out_specs=(P("ax", "tr", None), P("ax", "tr", None), P("ax", "tr", None)),
        check_vma=False,
    )
```

```python
import functools
import math

import jax
import jax.numpy as jnp
import ml_dtypes
import numpy as np
from jax import lax
from jax.experimental import pallas as pl
from jax.experimental.pallas import tpu as pltpu
from jax.sharding import PartitionSpec as P

COUPLE = 8.0
ALONG_ROW = 100.0
ACROSS_ROWS = 4000.0
MESH = pl.DeviceIdType.MESH
F32 = jnp.float32
BF16 = jnp.bfloat16


def halves(table):
    high = table.astype(np.float32).astype(ml_dtypes.bfloat16)
    low = (table - high.astype(np.float64)).astype(np.float32).astype(ml_dtypes.bfloat16)
    return np.stack([high, low])


def line_inverse(order_n, conduct):
    theta = 2.0 * math.asinh(0.5 / math.sqrt(conduct))
    i = np.arange(1, order_n + 1, dtype=np.float64)
    near = np.minimum(i[:, None], i[None, :])
    far = order_n + 1 - np.maximum(i[:, None], i[None, :])
    return np.sinh(near * theta) * np.sinh(far * theta) / (
        conduct * math.sinh(theta) * math.sinh((order_n + 1) * theta)
    )


class Across:
    def __init__(self, rows, blocks, conduct, group):
        self.rows = rows
        self.last = rows * blocks + 1
        self.theta = 2.0 * math.asinh(0.5 / math.sqrt(conduct))
        kappa = 1.0 / (2.0 * conduct * math.sinh(self.theta))
        a = np.arange(1, rows + 1, dtype=np.float64)
        block = kappa * np.exp(-np.abs(a[:, None] - a[None, :]) * self.theta)
        self.local = halves(np.kron(np.eye(group), block))
        self.pair = 0.5 / (conduct * math.sinh(self.theta) * math.sinh(self.last * self.theta))
        end = math.exp(-self.last * self.theta)
        self.near = -kappa / (1.0 - end**2)
        self.cross = kappa * end / (1.0 - end**2) * math.exp(-(self.last - rows) * self.theta)

    def fade_down(self, first):
        row = lax.broadcasted_iota(jnp.int32, (self.rows, 128), 0)
        return jnp.exp((row + first).astype(F32) * -self.theta)

    def fade_up(self, last):
        row = lax.broadcasted_iota(jnp.int32, (self.rows, 128), 0)
        return jnp.exp((self.rows - 1 + last - row).astype(F32) * -self.theta)

    def power(self, steps, lanes):
        tile = jnp.exp(jnp.full((8, 128), steps, jnp.int32).astype(F32) * self.theta)
        return jnp.concatenate([tile] * (lanes // 128), axis=1)

    def sums(self, block, to_last, to_first):
        rows, lanes = self.rows, to_last.shape[1]
        power = functools.partial(self.power, lanes=lanes)
        before = rows * block
        return (
            0.5 * (power(before + rows) * to_last - power(-before - 1) * to_first),
            0.5
            * (
                power(self.last - before - 1) * to_first
                - power(before + rows - self.last) * to_last
            ),
        )

    def fields(self, block, below, above, to_last, to_first):
        rows, lanes = self.rows, to_last.shape[1]
        power = functools.partial(self.power, lanes=lanes)
        before = rows * block
        return (
            self.pair * (power(self.last - before) * below - power(-before) * above)
            + self.cross * to_last
            + self.near * power(-2 * before - 1) * to_first,
            self.pair
            * (power(before + rows + 1) * above - power(before + rows + 1 - self.last) * below)
            + self.cross * to_first
            + self.near * power(2 * before + 2 * rows + 1 - 2 * self.last) * to_last,
        )


def dot3(a_high, a_low, b_high, b_low):
    dot = functools.partial(jnp.dot, preferred_element_type=F32)
    return dot(a_high, b_high) + (dot(a_low, b_high) + dot(a_high, b_low))


def split(value):
    high = value.astype(BF16)
    return high, (value - high.astype(F32)).astype(BF16)


def row_sums(values):
    values = [sum(v[i : i + 8] for i in range(8, v.shape[0], 8)) + v[:8] for v in values]
    row = lax.broadcasted_iota(jnp.int32, values[0].shape, 0)
    step = 4
    while step:
        low = (row & step) == 0
        count = len(values) // 2
        values = [
            jnp.where(low, a, pltpu.roll(b, step, 0)) + jnp.where(low, pltpu.roll(a, 8 - step, 0), b)
            for a, b in zip(values[:count], values[count:])
        ]
        step //= 2
    return values[0]


def exchange_kernel(
    n_ax,
    n_tr,
    across,
    solid_hbm,
    rate_hbm,
    inlet_hbm,
    along_hbm,
    local_hbm,
    gas,
    part,
    carry,
    solid,
    rate,
    inlet,
    along,
    local,
    cumul,
    particular,
    still,
    driven,
    right_hi,
    right_lo,
    mid_hi,
    mid_lo,
    pieces,
    maps,
    flows,
    inflow,
    own,
    sums,
    sums_in,
    twin_out,
    pairs,
    load_sem,
    send_sem,
    recv_sem,
):
    me_ax = lax.axis_index("ax")
    me_tr = lax.axis_index("tr")
    planes, rows, cols = solid.shape
    col_tiles = cols // 128
    half = planes // 2
    n_owner = pieces.shape[0]
    ring, place = me_ax // 8, lax.rem(me_ax, 8)
    wide = jnp.logical_and(ring < 2, place != 4)
    is_owner = jnp.logical_or(wide, jnp.logical_and(ring == 2, place < 2))
    my_piece = jnp.where(wide, ring * 7 + lax.rem(place + 3, 8), jnp.where(is_owner, 14 + place, 0))

    def owner_of(piece):
        wide_at = piece // 7 * 8 + lax.rem(lax.rem(piece, 7) + 5, 8)
        return jnp.where(piece < 14, wide_at, piece + 2)

    core = lax.rem(me_tr, 2)
    twin = me_tr + 1 - 2 * core

    first_rows, last_rows = pl.ds(0, rows // 2), pl.ds(rows // 2, rows // 2)
    loads = [
        pltpu.make_async_copy(source, target, load_sem.at[i])
        for i, (source, target) in enumerate(
            [
                (rate_hbm.at[:, first_rows], rate.at[:, first_rows]),
                (solid_hbm.at[:, first_rows], solid.at[:, first_rows]),
                (rate_hbm.at[:, last_rows], rate.at[:, last_rows]),
                (solid_hbm.at[:, last_rows], solid.at[:, last_rows]),
                (inlet_hbm, inlet),
                (local_hbm, local),
                (along_hbm, along),
            ]
        )
    ]
    for load in loads[:5]:
        load.start()

    barrier = pltpu.get_barrier_semaphore()

    def greet(ax, tr):
        pl.semaphore_signal(barrier, inc=1, device_id=(ax, tr), device_id_type=MESH)

    @pl.when(is_owner)
    def _():
        def one(k, _):
            greet(lax.rem(me_ax + k, n_ax), me_tr)
            return 0

        lax.fori_loop(1, n_ax, one, 0)

    def greet_tr(k, _):
        greet(me_ax, lax.rem(me_tr + k, n_tr))
        return 0

    lax.fori_loop(1, n_tr, greet_tr, 0)

    for g in range(2):
        loads[2 * g].wait()
        loads[2 * g + 1].wait()
        if g == 1:
            loads[4].wait()
            loads[5].start()
            loads[6].start()
        at = pl.ds(g * 16, 16)

        def plane(p, state, at=at):
            factor, offset = state
            r = rate[p, at, :].astype(F32)
            near_keep = pl.reciprocal(1.0 + r, approx=True)
            keep = near_keep * (2.0 - (1.0 + r) * near_keep)
            factor = factor * keep
            offset = (offset + r * solid[p, at, :]) * keep
            cumul[p, at, :] = factor
            particular[p, at, :] = offset
            return factor, offset

        factor, offset = lax.fori_loop(
            0,
            planes,
            plane,
            (jnp.ones((16, cols), F32), jnp.zeros((16, cols), F32)),
            unroll=True,
        )
        for h in range(2):
            for c in range(col_tiles):
                box = (slice(8 * h, 8 * h + 8), slice(128 * c, 128 * c + 128))
                q = (g * 2 + h) * col_tiles + c
                pieces[q, 0] = factor[box]
                pieces[q, 1] = offset[box]

    pl.semaphore_wait(barrier, jnp.where(is_owner, n_owner - 1, n_owner) + n_tr - 1)

    def send_map(k, _):
        piece = lax.rem(me_ax + k, n_owner)
        to = owner_of(piece)

        @pl.when(to != me_ax)
        def _():
            pltpu.make_async_remote_copy(
                src_ref=pieces.at[piece],
                dst_ref=maps.at[me_ax],
                send_sem=send_sem.at[0],
                recv_sem=recv_sem.at[0],
                device_id=(to, me_tr),
                device_id_type=MESH,
            ).start()

        return 0

    lax.fori_loop(0, n_owner, send_map, 0)

    to_last, to_first = across.fade_up(0), across.fade_down(0)

    def prepare(g, _):
        for c in range(col_tiles):
            lanes = pl.ds(128 * c, 128)
            values = []
            for j in range(half):
                p = g * half + j
                s = solid[p, :, lanes]
                r = COUPLE * rate[p, :, lanes].astype(F32)
                driven[p, :, lanes] = r * cumul[p, :, lanes]
                values.append(s + r * (particular[p, :, lanes] - s))
                still[p, :, lanes] = values[-1]
            own[g, 0, :, lanes] = row_sums([v * to_last for v in values])
            own[g, 1, :, lanes] = row_sums([v * to_first for v in values])
        return 0

    lax.fori_loop(0, 2, prepare, 0)

    def wait_for(ref, count, sem):
        box = ref.at[pl.ds(0, count)]
        pltpu.make_async_copy(box, box, sem).wait()

    def tile_of(ref, piece):
        return ref.at[
            pl.ds(pl.multiple_of(piece // col_tiles * 8, 8), 8),
            pl.ds(pl.multiple_of(lax.rem(piece, col_tiles) * 128, 128), 128),
        ]

    @pl.when(is_owner)
    def _():
        maps[me_ax] = pieces[my_piece]
        wait_for(maps, n_ax - 1, recv_sem.at[0])

        def march(k, state):
            flows[k] = state
            return maps[k, 0] * state + maps[k, 1]

        lax.fori_loop(0, n_ax, march, tile_of(inlet, my_piece)[...], unroll=True)

        def send_flow(k, _):
            to = lax.rem(k, 4) * 8 + k // 4

            @pl.when(to != me_ax)
            def _():
                pltpu.make_async_remote_copy(
                    src_ref=flows.at[to],
                    dst_ref=tile_of(inflow, my_piece),
                    send_sem=send_sem.at[1],
                    recv_sem=recv_sem.at[1],
                    device_id=(to, me_tr),
                    device_id_type=MESH,
                ).start()

            return 0

        lax.fori_loop(0, n_ax, send_flow, 0)
        tile_of(inflow, my_piece)[...] = flows[me_ax]
        wait_for(flows, n_owner - 1, recv_sem.at[1])

    @pl.when(jnp.logical_not(is_owner))
    def _():
        wait_for(flows, n_owner, recv_sem.at[1])

    def send_sum(to):
        pltpu.make_async_remote_copy(
            src_ref=sums.at[lax.rem(to, 2), (to < me_tr).astype(jnp.int32)],
            dst_ref=sums_in.at[me_tr],
            send_sem=send_sem.at[2],
            recv_sem=recv_sem.at[2],
            device_id=(me_ax, to),
            device_id_type=MESH,
        ).start()

    def add_inflow(g, _):
        for c in range(col_tiles):
            lanes = pl.ds(128 * c, 128)
            flow = inflow[:, lanes]
            down, up = flow * to_last, flow * to_first
            values = [driven[g * half + j, :, lanes] for j in range(half)]
            last = own[g, 0, :, lanes] + row_sums([v * down for v in values])
            start = own[g, 1, :, lanes] + row_sums([v * up for v in values])
            own[g, 0, :, lanes], own[g, 1, :, lanes] = last, start
            sums[g, 0, :, lanes], sums[g, 1, :, lanes] = across.sums(me_tr, last, start)
        return 0

    lax.fori_loop(0, 2, add_inflow, 0)

    def send(to, _):
        @pl.when(to != me_tr)
        def _():
            send_sum(to)

        return 0

    lax.fori_loop(0, n_tr, send, 0)
    sums_in[me_tr] = sums[core, core]

    def finish_plane(p, _):
        gas[p] = particular[p] + cumul[p] * inflow[...]
        at = pl.ds(pl.multiple_of(p * rows, rows), rows)
        right_hi[at, :], right_lo[at, :] = split(still[p] + driven[p] * inflow[...])
        return 0

    lax.fori_loop(0, planes, finish_plane, 0, unroll=2)

    loads[5].wait()
    loads[6].wait()
    group = local.shape[1]

    def own_solve(g, _):
        at = pl.ds(pl.multiple_of(g * group, group), group)
        mid = dot3(local[0], local[1], right_hi[at, :], right_lo[at, :])
        mid_hi[at, :], mid_lo[at, :] = split(mid)
        part[at, :] = dot3(mid_hi[at, :], mid_lo[at, :], along[0], along[1])
        return 0

    lax.fori_loop(0, planes * rows // group, own_solve, 0)

    wait_for(sums_in, n_tr - 1, recv_sem.at[2])

    nothing = jnp.zeros((half, cols), F32)

    def add(k, totals):
        value = sums_in[k]
        return tuple(
            total + jnp.where(test, value, 0.0)
            for total, test in zip(totals, (k < me_tr, k > me_tr, k < twin, k > twin))
        )

    mine = lax.fori_loop(0, n_tr, add, (nothing,) * 4, unroll=True)
    twin_out[0], twin_out[1] = mine[2], mine[3]
    to_twin = pltpu.make_async_remote_copy(
        src_ref=twin_out,
        dst_ref=pairs.at[core],
        send_sem=send_sem.at[3],
        recv_sem=recv_sem.at[3],
        device_id=(me_ax, twin),
        device_id_type=MESH,
    )
    to_twin.start()
    pairs[core, 0], pairs[core, 1] = mine[0], mine[1]

    to_twin.wait_recv()
    fields = []
    for g in range(2):
        fields.extend(
            across.fields(me_tr, pairs[g, 0], pairs[g, 1], own[g, 0], own[g, 1])
        )
    end_hi, end_lo = split(jnp.concatenate(fields, axis=0))
    carry[...] = dot3(end_hi, end_lo, along[0], along[1])

    to_twin.wait_send()
    wait_for(sums_in, n_tr - 1, send_sem.at[2])

    @pl.when(is_owner)
    def _():
        wait_for(pieces, n_owner - 1, send_sem.at[0])
        wait_for(flows, n_ax - 1, send_sem.at[1])

    @pl.when(jnp.logical_not(is_owner))
    def _():
        wait_for(pieces, n_owner, send_sem.at[0])


def finish_kernel(across, gas, part, carry, gas_hbm, solid_hbm, gap_hbm, solid, gap, store_sem):
    planes, rows, cols = gas.shape
    half = planes // 2
    gas_store = pltpu.make_async_copy(gas, gas_hbm, store_sem.at[0, 0])
    gas_store.start()
    before = jnp.concatenate([across.fade_down(1)] * (cols // 128), axis=1)
    after = jnp.concatenate([across.fade_up(1)] * (cols // 128), axis=1)
    stores = []
    for p in range(planes):
        row = p // half * planes + p % half
        new = part[p] + (
            before * jnp.broadcast_to(carry[row : row + 1, :], (rows, cols))
            + after * jnp.broadcast_to(carry[row + half : row + half + 1, :], (rows, cols))
        )
        solid[p] = new
        gap[p] = gas[p] - new
        if p % 2 == 1:
            for i, (source, target) in enumerate(((solid, solid_hbm), (gap, gap_hbm))):
                box = pl.ds(p - 1, 2)
                stores.append(
                    pltpu.make_async_copy(
                        source.at[box], target.at[box], store_sem.at[1 + i, p // 2]
                    )
                )
                stores[-1].start()
    gas_store.wait()
    for store in stores:
        store.wait()


def far(value):
    return pltpu.with_memory_space_constraint(value, pltpu.HBM)


def per_device(n_ax, n_tr, solid_old, gas_rate, gas_inlet):
    planes, rows, cols = solid_old.shape
    across = Across(rows, n_tr, ACROSS_ROWS, 8)
    along = halves(line_inverse(cols, ALONG_ROW).T)
    cells = planes * rows
    half = planes // 2
    pieces = (rows // 8) * (cols // 128)
    field = (planes, rows, cols)
    anywhere = pl.BlockSpec(memory_space=pl.ANY)
    near = pl.BlockSpec(memory_space=pltpu.VMEM)
    gas, part, carry = pl.pallas_call(
        functools.partial(exchange_kernel, n_ax, n_tr, across),
        out_shape=(
            pltpu.VMEM(field, F32),
            pltpu.VMEM((cells, cols), F32),
            pltpu.VMEM((2 * planes, cols), F32),
        ),
        in_specs=[anywhere] * 5,
        out_specs=[near] * 3,
        scratch_shapes=[
            pltpu.VMEM(field, F32),
            pltpu.VMEM(field, BF16),
            pltpu.VMEM((rows, cols), F32),
            pltpu.VMEM((2, cols, cols), BF16),
            pltpu.VMEM(across.local.shape, BF16),
            pltpu.VMEM(field, F32),
            pltpu.VMEM(field, F32),
            pltpu.VMEM(field, F32),
            pltpu.VMEM(field, F32),
            pltpu.VMEM((cells, cols), BF16),
            pltpu.VMEM((cells, cols), BF16),
            pltpu.VMEM((cells, cols), BF16),
            pltpu.VMEM((cells, cols), BF16),
            pltpu.VMEM((pieces, 2, 8, 128), F32),
            pltpu.VMEM((n_ax, 2, 8, 128), F32),
            pltpu.VMEM((n_ax, 8, 128), F32),
            pltpu.VMEM((rows, cols), F32),
            pltpu.VMEM((2, 2, half, cols), F32),
            pltpu.VMEM((2, 2, half, cols), F32),
            pltpu.VMEM((n_tr, half, cols), F32),
            pltpu.VMEM((2, half, cols), F32),
            pltpu.VMEM((2, 2, half, cols), F32),
            pltpu.SemaphoreType.DMA((7,)),
            pltpu.SemaphoreType.DMA((4,)),
            pltpu.SemaphoreType.DMA((4,)),
        ],
        compiler_params=pltpu.CompilerParams(
            collective_id=0, has_side_effects=True, vmem_limit_bytes=32 * 2**20
        ),
        name="exchange",
    )(*map(far, (solid_old, gas_rate, gas_inlet, jnp.asarray(along), jnp.asarray(across.local))))

    shape = jax.ShapeDtypeStruct(field, F32)
    return pl.pallas_call(
        functools.partial(finish_kernel, across),
        out_shape=(shape, shape, shape),
        in_specs=[near] * 3,
        out_specs=[anywhere] * 3,
        scratch_shapes=[
            pltpu.VMEM(field, F32),
            pltpu.VMEM(field, F32),
            pltpu.SemaphoreType.DMA((3, planes // 2)),
        ],
        compiler_params=pltpu.CompilerParams(vmem_limit_bytes=16 * 2**20),
        name="finish",
    )(gas, part.reshape(field), carry)


def solution(mesh):
    n_ax, n_tr = mesh.shape["ax"], mesh.shape["tr"]
    return jax.shard_map(
        functools.partial(per_device, n_ax, n_tr),
        mesh=mesh,
        in_specs=(P("ax", "tr", None), P("ax", "tr", None), P("tr", None)),
        out_specs=(P("ax", "tr", None), P("ax", "tr", None), P("ax", "tr", None)),
        check_vma=False,
    )
```

```python
import functools
import math

import jax
import jax.numpy as jnp
import ml_dtypes
import numpy as np
from jax import lax
from jax.experimental import pallas as pl
from jax.experimental.pallas import tpu as pltpu
from jax.sharding import PartitionSpec as P

COUPLE = 8.0
ALONG_ROW = 100.0
ACROSS_ROWS = 4000.0
MESH = pl.DeviceIdType.MESH
F32 = jnp.float32
BF16 = jnp.bfloat16


def halves(table):
    high = table.astype(np.float32).astype(ml_dtypes.bfloat16)
    low = (table - high.astype(np.float64)).astype(np.float32).astype(ml_dtypes.bfloat16)
    return np.stack([high, low])


def line_inverse(order_n, conduct):
    theta = 2.0 * math.asinh(0.5 / math.sqrt(conduct))
    i = np.arange(1, order_n + 1, dtype=np.float64)
    near = np.minimum(i[:, None], i[None, :])
    far = order_n + 1 - np.maximum(i[:, None], i[None, :])
    return np.sinh(near * theta) * np.sinh(far * theta) / (
        conduct * math.sinh(theta) * math.sinh((order_n + 1) * theta)
    )


class Across:
    def __init__(self, rows, blocks, conduct, group):
        self.rows = rows
        self.last = rows * blocks + 1
        self.theta = 2.0 * math.asinh(0.5 / math.sqrt(conduct))
        kappa = 1.0 / (2.0 * conduct * math.sinh(self.theta))
        a = np.arange(1, rows + 1, dtype=np.float64)
        block = kappa * np.exp(-np.abs(a[:, None] - a[None, :]) * self.theta)
        self.local = halves(np.kron(np.eye(group), block))
        self.pair = 0.5 / (conduct * math.sinh(self.theta) * math.sinh(self.last * self.theta))
        end = math.exp(-self.last * self.theta)
        self.near = -kappa / (1.0 - end**2)
        self.cross = kappa * end / (1.0 - end**2) * math.exp(-(self.last - rows) * self.theta)

    def fade_down(self, first):
        row = lax.broadcasted_iota(jnp.int32, (self.rows, 128), 0)
        return jnp.exp((row + first).astype(F32) * -self.theta)

    def fade_up(self, last):
        row = lax.broadcasted_iota(jnp.int32, (self.rows, 128), 0)
        return jnp.exp((self.rows - 1 + last - row).astype(F32) * -self.theta)

    def power(self, steps, lanes):
        tile = jnp.exp(jnp.full((8, 128), steps, jnp.int32).astype(F32) * self.theta)
        return jnp.concatenate([tile] * (lanes // 128), axis=1)

    def sums(self, block, to_last, to_first):
        rows, lanes = self.rows, to_last.shape[1]
        power = functools.partial(self.power, lanes=lanes)
        before = rows * block
        return (
            0.5 * (power(before + rows) * to_last - power(-before - 1) * to_first),
            0.5
            * (
                power(self.last - before - 1) * to_first
                - power(before + rows - self.last) * to_last
            ),
        )

    def fields(self, block, below, above, to_last, to_first):
        rows, lanes = self.rows, to_last.shape[1]
        power = functools.partial(self.power, lanes=lanes)
        before = rows * block
        return (
            self.pair * (power(self.last - before) * below - power(-before) * above)
            + self.cross * to_last
            + self.near * power(-2 * before - 1) * to_first,
            self.pair
            * (power(before + rows + 1) * above - power(before + rows + 1 - self.last) * below)
            + self.cross * to_first
            + self.near * power(2 * before + 2 * rows + 1 - 2 * self.last) * to_last,
        )


def dot3(a_high, a_low, b_high, b_low):
    dot = functools.partial(jnp.dot, preferred_element_type=F32)
    return dot(a_high, b_high) + (dot(a_low, b_high) + dot(a_high, b_low))


def split(value):
    high = value.astype(BF16)
    return high, (value - high.astype(F32)).astype(BF16)


def row_sums(values):
    values = [sum(v[i : i + 8] for i in range(8, v.shape[0], 8)) + v[:8] for v in values]
    row = lax.broadcasted_iota(jnp.int32, values[0].shape, 0)
    step = 4
    while step:
        low = (row & step) == 0
        count = len(values) // 2
        values = [
            jnp.where(low, a, pltpu.roll(b, step, 0)) + jnp.where(low, pltpu.roll(a, 8 - step, 0), b)
            for a, b in zip(values[:count], values[count:])
        ]
        step //= 2
    return values[0]


def exchange_kernel(
    n_ax,
    n_tr,
    across,
    solid_hbm,
    rate_hbm,
    inlet_hbm,
    along_hbm,
    local_hbm,
    gas,
    part,
    carry,
    solid,
    rate,
    inlet,
    along,
    local,
    cumul,
    particular,
    still,
    driven,
    right_hi,
    right_lo,
    mid_hi,
    mid_lo,
    pieces,
    maps,
    flows,
    inflow,
    own,
    sums,
    sums_in,
    twin_out,
    pairs,
    load_sem,
    send_sem,
    recv_sem,
):
    me_ax = lax.axis_index("ax")
    me_tr = lax.axis_index("tr")
    planes, rows, cols = solid.shape
    col_tiles = cols // 128
    half = planes // 2
    n_owner = pieces.shape[0]
    ring, place = me_ax // 8, lax.rem(me_ax, 8)
    wide = jnp.logical_and(ring < 2, place != 4)
    is_owner = jnp.logical_or(wide, jnp.logical_and(ring == 2, place < 2))
    my_piece = jnp.where(wide, ring * 7 + lax.rem(place + 3, 8), jnp.where(is_owner, 14 + place, 0))

    def owner_of(piece):
        wide_at = piece // 7 * 8 + lax.rem(lax.rem(piece, 7) + 5, 8)
        return jnp.where(piece < 14, wide_at, piece + 2)

    core = lax.rem(me_tr, 2)
    twin = me_tr + 1 - 2 * core

    barrier = pltpu.get_barrier_semaphore()

    def greet(ax, tr):
        pl.semaphore_signal(barrier, inc=1, device_id=(ax, tr), device_id_type=MESH)

    @pl.when(is_owner)
    def _():
        def one(k, _):
            to = lax.rem(me_ax + n_ax // 2 - 4 + k, n_ax)

            @pl.when(to != me_ax)
            def _():
                greet(to, me_tr)

            return 0

        lax.fori_loop(0, n_ax, one, 0)

    first_rows, last_rows = pl.ds(0, rows // 2), pl.ds(rows // 2, rows // 2)
    loads = [
        pltpu.make_async_copy(source, target, load_sem.at[i])
        for i, (source, target) in enumerate(
            [
                (rate_hbm.at[:, first_rows], rate.at[:, first_rows]),
                (solid_hbm.at[:, first_rows], solid.at[:, first_rows]),
                (rate_hbm.at[:, last_rows], rate.at[:, last_rows]),
                (solid_hbm.at[:, last_rows], solid.at[:, last_rows]),
                (inlet_hbm, inlet),
                (local_hbm, local),
                (along_hbm, along),
            ]
        )
    ]
    for load in loads[:5]:
        load.start()

    def greet_tr(k, _):
        greet(me_ax, lax.rem(me_tr + k, n_tr))
        return 0

    lax.fori_loop(1, n_tr, greet_tr, 0)

    for g in range(2):
        loads[2 * g].wait()
        loads[2 * g + 1].wait()
        if g == 1:
            loads[4].wait()
            loads[5].start()
            loads[6].start()
        at = pl.ds(g * 16, 16)

        def plane(p, state, at=at):
            factor, offset = state
            r = rate[p, at, :].astype(F32)
            near_keep = pl.reciprocal(1.0 + r, approx=True)
            keep = near_keep * (2.0 - (1.0 + r) * near_keep)
            factor = factor * keep
            offset = (offset + r * solid[p, at, :]) * keep
            cumul[p, at, :] = factor
            particular[p, at, :] = offset
            return factor, offset

        factor, offset = lax.fori_loop(
            0,
            planes,
            plane,
            (jnp.ones((16, cols), F32), jnp.zeros((16, cols), F32)),
            unroll=True,
        )
        for h in range(2):
            for c in range(col_tiles):
                box = (slice(8 * h, 8 * h + 8), slice(128 * c, 128 * c + 128))
                q = (g * 2 + h) * col_tiles + c
                pieces[q, 0] = factor[box]
                pieces[q, 1] = offset[box]

    pl.semaphore_wait(barrier, jnp.where(is_owner, n_owner - 1, n_owner) + n_tr - 1)

    def send_map(k, _):
        piece = lax.rem(me_ax + k, n_owner)
        to = owner_of(piece)

        @pl.when(to != me_ax)
        def _():
            pltpu.make_async_remote_copy(
                src_ref=pieces.at[piece],
                dst_ref=maps.at[me_ax],
                send_sem=send_sem.at[0],
                recv_sem=recv_sem.at[0],
                device_id=(to, me_tr),
                device_id_type=MESH,
            ).start()

        return 0

    lax.fori_loop(0, n_owner, send_map, 0)

    to_last, to_first = across.fade_up(0), across.fade_down(0)

    def prepare(g, _):
        for c in range(col_tiles):
            lanes = pl.ds(128 * c, 128)
            values = []
            for j in range(half):
                p = g * half + j
                s = solid[p, :, lanes]
                r = COUPLE * rate[p, :, lanes].astype(F32)
                driven[p, :, lanes] = r * cumul[p, :, lanes]
                values.append(s + r * (particular[p, :, lanes] - s))
                still[p, :, lanes] = values[-1]
            own[g, 0, :, lanes] = row_sums([v * to_last for v in values])
            own[g, 1, :, lanes] = row_sums([v * to_first for v in values])
        return 0

    lax.fori_loop(0, 2, prepare, 0)

    def wait_for(ref, count, sem):
        box = ref.at[pl.ds(0, count)]
        pltpu.make_async_copy(box, box, sem).wait()

    def tile_of(ref, piece):
        return ref.at[
            pl.ds(pl.multiple_of(piece // col_tiles * 8, 8), 8),
            pl.ds(pl.multiple_of(lax.rem(piece, col_tiles) * 128, 128), 128),
        ]

    @pl.when(is_owner)
    def _():
        maps[me_ax] = pieces[my_piece]
        wait_for(maps, n_ax - 1, recv_sem.at[0])

        def march(k, state):
            flows[k] = state
            return maps[k, 0] * state + maps[k, 1]

        lax.fori_loop(0, n_ax, march, tile_of(inlet, my_piece)[...], unroll=True)

        def send_flow(k, _):
            to = lax.rem(k, 4) * 8 + k // 4

            @pl.when(to != me_ax)
            def _():
                pltpu.make_async_remote_copy(
                    src_ref=flows.at[to],
                    dst_ref=tile_of(inflow, my_piece),
                    send_sem=send_sem.at[1],
                    recv_sem=recv_sem.at[1],
                    device_id=(to, me_tr),
                    device_id_type=MESH,
                ).start()

            return 0

        lax.fori_loop(0, n_ax, send_flow, 0)
        tile_of(inflow, my_piece)[...] = flows[me_ax]
        wait_for(flows, n_owner - 1, recv_sem.at[1])

    @pl.when(jnp.logical_not(is_owner))
    def _():
        wait_for(flows, n_owner, recv_sem.at[1])

    def send_sum(to):
        pltpu.make_async_remote_copy(
            src_ref=sums.at[lax.rem(to, 2), (to < me_tr).astype(jnp.int32)],
            dst_ref=sums_in.at[me_tr],
            send_sem=send_sem.at[2],
            recv_sem=recv_sem.at[2],
            device_id=(me_ax, to),
            device_id_type=MESH,
        ).start()

    def add_inflow(g, _):
        for c in range(col_tiles):
            lanes = pl.ds(128 * c, 128)
            flow = inflow[:, lanes]
            down, up = flow * to_last, flow * to_first
            values = [driven[g * half + j, :, lanes] for j in range(half)]
            last = own[g, 0, :, lanes] + row_sums([v * down for v in values])
            start = own[g, 1, :, lanes] + row_sums([v * up for v in values])
            own[g, 0, :, lanes], own[g, 1, :, lanes] = last, start
            sums[g, 0, :, lanes], sums[g, 1, :, lanes] = across.sums(me_tr, last, start)
        return 0

    lax.fori_loop(0, 2, add_inflow, 0)

    def send(to, _):
        @pl.when(to != me_tr)
        def _():
            send_sum(to)

        return 0

    lax.fori_loop(0, n_tr, send, 0)
    sums_in[me_tr] = sums[core, core]

    def finish_plane(p, _):
        gas[p] = particular[p] + cumul[p] * inflow[...]
        at = pl.ds(pl.multiple_of(p * rows, rows), rows)
        right_hi[at, :], right_lo[at, :] = split(still[p] + driven[p] * inflow[...])
        return 0

    lax.fori_loop(0, planes, finish_plane, 0, unroll=2)

    loads[5].wait()
    loads[6].wait()
    group = local.shape[1]

    def own_solve(g, _):
        at = pl.ds(pl.multiple_of(g * group, group), group)
        mid = dot3(local[0], local[1], right_hi[at, :], right_lo[at, :])
        mid_hi[at, :], mid_lo[at, :] = split(mid)
        part[at, :] = dot3(mid_hi[at, :], mid_lo[at, :], along[0], along[1])
        return 0

    lax.fori_loop(0, planes * rows // group, own_solve, 0)

    wait_for(sums_in, n_tr - 1, recv_sem.at[2])

    nothing = jnp.zeros((half, cols), F32)

    def add(k, totals):
        value = sums_in[k]
        return tuple(
            total + jnp.where(test, value, 0.0)
            for total, test in zip(totals, (k < me_tr, k > me_tr, k < twin, k > twin))
        )

    mine = lax.fori_loop(0, n_tr, add, (nothing,) * 4, unroll=True)
    twin_out[0], twin_out[1] = mine[2], mine[3]
    to_twin = pltpu.make_async_remote_copy(
        src_ref=twin_out,
        dst_ref=pairs.at[core],
        send_sem=send_sem.at[3],
        recv_sem=recv_sem.at[3],
        device_id=(me_ax, twin),
        device_id_type=MESH,
    )
    to_twin.start()
    pairs[core, 0], pairs[core, 1] = mine[0], mine[1]

    to_twin.wait_recv()
    fields = []
    for g in range(2):
        fields.extend(
            across.fields(me_tr, pairs[g, 0], pairs[g, 1], own[g, 0], own[g, 1])
        )
    end_hi, end_lo = split(jnp.concatenate(fields, axis=0))
    carry[...] = dot3(end_hi, end_lo, along[0], along[1])

    to_twin.wait_send()
    wait_for(sums_in, n_tr - 1, send_sem.at[2])

    @pl.when(is_owner)
    def _():
        wait_for(pieces, n_owner - 1, send_sem.at[0])
        wait_for(flows, n_ax - 1, send_sem.at[1])

    @pl.when(jnp.logical_not(is_owner))
    def _():
        wait_for(pieces, n_owner, send_sem.at[0])


def finish_kernel(across, gas, part, carry, gas_hbm, solid_hbm, gap_hbm, solid, gap, store_sem):
    planes, rows, cols = gas.shape
    half = planes // 2
    gas_store = pltpu.make_async_copy(gas, gas_hbm, store_sem.at[0, 0])
    gas_store.start()
    before = jnp.concatenate([across.fade_down(1)] * (cols // 128), axis=1)
    after = jnp.concatenate([across.fade_up(1)] * (cols // 128), axis=1)
    stores = []
    for p in range(planes):
        row = p // half * planes + p % half
        new = part[p] + (
            before * jnp.broadcast_to(carry[row : row + 1, :], (rows, cols))
            + after * jnp.broadcast_to(carry[row + half : row + half + 1, :], (rows, cols))
        )
        solid[p] = new
        gap[p] = gas[p] - new
        if p % 2 == 1:
            for i, (source, target) in enumerate(((solid, solid_hbm), (gap, gap_hbm))):
                box = pl.ds(p - 1, 2)
                stores.append(
                    pltpu.make_async_copy(
                        source.at[box], target.at[box], store_sem.at[1 + i, p // 2]
                    )
                )
                stores[-1].start()
    gas_store.wait()
    for store in stores:
        store.wait()


def far(value):
    return pltpu.with_memory_space_constraint(value, pltpu.HBM)


def per_device(n_ax, n_tr, solid_old, gas_rate, gas_inlet):
    planes, rows, cols = solid_old.shape
    across = Across(rows, n_tr, ACROSS_ROWS, 8)
    along = halves(line_inverse(cols, ALONG_ROW).T)
    cells = planes * rows
    half = planes // 2
    pieces = (rows // 8) * (cols // 128)
    field = (planes, rows, cols)
    anywhere = pl.BlockSpec(memory_space=pl.ANY)
    near = pl.BlockSpec(memory_space=pltpu.VMEM)
    gas, part, carry = pl.pallas_call(
        functools.partial(exchange_kernel, n_ax, n_tr, across),
        out_shape=(
            pltpu.VMEM(field, F32),
            pltpu.VMEM((cells, cols), F32),
            pltpu.VMEM((2 * planes, cols), F32),
        ),
        in_specs=[anywhere] * 5,
        out_specs=[near] * 3,
        scratch_shapes=[
            pltpu.VMEM(field, F32),
            pltpu.VMEM(field, BF16),
            pltpu.VMEM((rows, cols), F32),
            pltpu.VMEM((2, cols, cols), BF16),
            pltpu.VMEM(across.local.shape, BF16),
            pltpu.VMEM(field, F32),
            pltpu.VMEM(field, F32),
            pltpu.VMEM(field, F32),
            pltpu.VMEM(field, F32),
            pltpu.VMEM((cells, cols), BF16),
            pltpu.VMEM((cells, cols), BF16),
            pltpu.VMEM((cells, cols), BF16),
            pltpu.VMEM((cells, cols), BF16),
            pltpu.VMEM((pieces, 2, 8, 128), F32),
            pltpu.VMEM((n_ax, 2, 8, 128), F32),
            pltpu.VMEM((n_ax, 8, 128), F32),
            pltpu.VMEM((rows, cols), F32),
            pltpu.VMEM((2, 2, half, cols), F32),
            pltpu.VMEM((2, 2, half, cols), F32),
            pltpu.VMEM((n_tr, half, cols), F32),
            pltpu.VMEM((2, half, cols), F32),
            pltpu.VMEM((2, 2, half, cols), F32),
            pltpu.SemaphoreType.DMA((7,)),
            pltpu.SemaphoreType.DMA((4,)),
            pltpu.SemaphoreType.DMA((4,)),
        ],
        compiler_params=pltpu.CompilerParams(
            collective_id=0, has_side_effects=True, vmem_limit_bytes=32 * 2**20
        ),
        name="exchange",
    )(*map(far, (solid_old, gas_rate, gas_inlet, jnp.asarray(along), jnp.asarray(across.local))))

    shape = jax.ShapeDtypeStruct(field, F32)
    return pl.pallas_call(
        functools.partial(finish_kernel, across),
        out_shape=(shape, shape, shape),
        in_specs=[near] * 3,
        out_specs=[anywhere] * 3,
        scratch_shapes=[
            pltpu.VMEM(field, F32),
            pltpu.VMEM(field, F32),
            pltpu.SemaphoreType.DMA((3, planes // 2)),
        ],
        compiler_params=pltpu.CompilerParams(vmem_limit_bytes=16 * 2**20),
        name="finish",
    )(gas, part.reshape(field), carry)


def solution(mesh):
    n_ax, n_tr = mesh.shape["ax"], mesh.shape["tr"]
    return jax.shard_map(
        functools.partial(per_device, n_ax, n_tr),
        mesh=mesh,
        in_specs=(P("ax", "tr", None), P("ax", "tr", None), P("tr", None)),
        out_specs=(P("ax", "tr", None), P("ax", "tr", None), P("ax", "tr", None)),
        check_vma=False,
    )
```

```python
import functools
import math

import jax
import jax.numpy as jnp
import ml_dtypes
import numpy as np
from jax import lax
from jax.experimental import pallas as pl
from jax.experimental.pallas import tpu as pltpu
from jax.sharding import PartitionSpec as P

COUPLE = 8.0
ALONG_ROW = 100.0
ACROSS_ROWS = 4000.0
MESH = pl.DeviceIdType.MESH
F32 = jnp.float32
BF16 = jnp.bfloat16


def halves(table):
    high = table.astype(np.float32).astype(ml_dtypes.bfloat16)
    low = (table - high.astype(np.float64)).astype(np.float32).astype(ml_dtypes.bfloat16)
    return np.stack([high, low])


def line_inverse(order_n, conduct):
    theta = 2.0 * math.asinh(0.5 / math.sqrt(conduct))
    i = np.arange(1, order_n + 1, dtype=np.float64)
    near = np.minimum(i[:, None], i[None, :])
    far = order_n + 1 - np.maximum(i[:, None], i[None, :])
    return np.sinh(near * theta) * np.sinh(far * theta) / (
        conduct * math.sinh(theta) * math.sinh((order_n + 1) * theta)
    )


class Across:
    def __init__(self, rows, blocks, conduct, group):
        self.rows = rows
        self.last = rows * blocks + 1
        self.theta = 2.0 * math.asinh(0.5 / math.sqrt(conduct))
        kappa = 1.0 / (2.0 * conduct * math.sinh(self.theta))
        a = np.arange(1, rows + 1, dtype=np.float64)
        block = kappa * np.exp(-np.abs(a[:, None] - a[None, :]) * self.theta)
        self.local = halves(np.kron(np.eye(group), block))
        self.pair = 0.5 / (conduct * math.sinh(self.theta) * math.sinh(self.last * self.theta))
        end = math.exp(-self.last * self.theta)
        self.near = -kappa / (1.0 - end**2)
        self.cross = kappa * end / (1.0 - end**2) * math.exp(-(self.last - rows) * self.theta)

    def fade_down(self, first):
        row = lax.broadcasted_iota(jnp.int32, (self.rows, 128), 0)
        return jnp.exp((row + first).astype(F32) * -self.theta)

    def fade_up(self, last):
        row = lax.broadcasted_iota(jnp.int32, (self.rows, 128), 0)
        return jnp.exp((self.rows - 1 + last - row).astype(F32) * -self.theta)

    def power(self, steps, lanes):
        tile = jnp.exp(jnp.full((8, 128), steps, jnp.int32).astype(F32) * self.theta)
        return jnp.concatenate([tile] * (lanes // 128), axis=1)

    def sums(self, block, to_last, to_first):
        rows, lanes = self.rows, to_last.shape[1]
        power = functools.partial(self.power, lanes=lanes)
        before = rows * block
        return (
            0.5 * (power(before + rows) * to_last - power(-before - 1) * to_first),
            0.5
            * (
                power(self.last - before - 1) * to_first
                - power(before + rows - self.last) * to_last
            ),
        )

    def fields(self, block, below, above, to_last, to_first):
        rows, lanes = self.rows, to_last.shape[1]
        power = functools.partial(self.power, lanes=lanes)
        before = rows * block
        return (
            self.pair * (power(self.last - before) * below - power(-before) * above)
            + self.cross * to_last
            + self.near * power(-2 * before - 1) * to_first,
            self.pair
            * (power(before + rows + 1) * above - power(before + rows + 1 - self.last) * below)
            + self.cross * to_first
            + self.near * power(2 * before + 2 * rows + 1 - 2 * self.last) * to_last,
        )


def dot3(a_high, a_low, b_high, b_low):
    dot = functools.partial(jnp.dot, preferred_element_type=F32)
    return dot(a_high, b_high) + (dot(a_low, b_high) + dot(a_high, b_low))


def split(value):
    high = value.astype(BF16)
    return high, (value - high.astype(F32)).astype(BF16)


def row_sums(values):
    values = [sum(v[i : i + 8] for i in range(8, v.shape[0], 8)) + v[:8] for v in values]
    row = lax.broadcasted_iota(jnp.int32, values[0].shape, 0)
    step = 4
    while step:
        low = (row & step) == 0
        count = len(values) // 2
        values = [
            jnp.where(low, a, pltpu.roll(b, step, 0)) + jnp.where(low, pltpu.roll(a, 8 - step, 0), b)
            for a, b in zip(values[:count], values[count:])
        ]
        step //= 2
    return values[0]


def exchange_kernel(
    n_ax,
    n_tr,
    across,
    solid_hbm,
    rate_hbm,
    inlet_hbm,
    along_hbm,
    local_hbm,
    gas,
    part,
    carry,
    solid,
    rate,
    inlet,
    along,
    local,
    cumul,
    particular,
    still,
    driven,
    right_hi,
    right_lo,
    mid_hi,
    mid_lo,
    pieces,
    maps,
    flows,
    inflow,
    own,
    sums,
    sums_in,
    twin_out,
    pairs,
    load_sem,
    send_sem,
    recv_sem,
):
    me_ax = lax.axis_index("ax")
    me_tr = lax.axis_index("tr")
    planes, rows, cols = solid.shape
    col_tiles = cols // 128
    half = planes // 2
    n_owner = pieces.shape[0]
    ring, place = me_ax // 8, lax.rem(me_ax, 8)
    wide = jnp.logical_and(ring < 2, place != 4)
    is_owner = jnp.logical_or(wide, jnp.logical_and(ring == 2, place < 2))
    my_piece = jnp.where(wide, ring * 7 + lax.rem(place + 3, 8), jnp.where(is_owner, 14 + place, 0))

    def owner_of(piece):
        wide_at = piece // 7 * 8 + lax.rem(lax.rem(piece, 7) + 5, 8)
        return jnp.where(piece < 14, wide_at, piece + 2)

    core = lax.rem(me_tr, 2)
    twin = me_tr + 1 - 2 * core

    barrier = pltpu.get_barrier_semaphore()

    def greet(ax, tr):
        pl.semaphore_signal(barrier, inc=1, device_id=(ax, tr), device_id_type=MESH)

    @pl.when(is_owner)
    def _():
        def one(k, _):
            to = lax.rem(me_ax + n_ax // 2 - 4 + k, n_ax)

            @pl.when(to != me_ax)
            def _():
                greet(to, me_tr)

            return 0

        lax.fori_loop(0, n_ax, one, 0)

    first_rows, last_rows = pl.ds(0, rows // 2), pl.ds(rows // 2, rows // 2)
    loads = [
        pltpu.make_async_copy(source, target, load_sem.at[i])
        for i, (source, target) in enumerate(
            [
                (rate_hbm.at[:, first_rows], rate.at[:, first_rows]),
                (solid_hbm.at[:, first_rows], solid.at[:, first_rows]),
                (rate_hbm.at[:, last_rows], rate.at[:, last_rows]),
                (solid_hbm.at[:, last_rows], solid.at[:, last_rows]),
                (inlet_hbm, inlet),
                (local_hbm, local),
                (along_hbm, along),
            ]
        )
    ]
    for load in loads[:5]:
        load.start()

    def greet_tr(k, _):
        greet(me_ax, lax.rem(me_tr + k, n_tr))
        return 0

    lax.fori_loop(1, n_tr, greet_tr, 0)

    for g in range(2):
        loads[2 * g].wait()
        loads[2 * g + 1].wait()
        if g == 1:
            loads[4].wait()
            loads[5].start()
            loads[6].start()
        at = pl.ds(g * 16, 16)

        def plane(p, state, at=at):
            factor, offset = state
            r = rate[p, at, :].astype(F32)
            near_keep = pl.reciprocal(1.0 + r, approx=True)
            keep = near_keep * (2.0 - (1.0 + r) * near_keep)
            factor = factor * keep
            offset = (offset + r * solid[p, at, :]) * keep
            cumul[p, at, :] = factor
            particular[p, at, :] = offset
            return factor, offset

        factor, offset = lax.fori_loop(
            0,
            planes,
            plane,
            (jnp.ones((16, cols), F32), jnp.zeros((16, cols), F32)),
            unroll=True,
        )
        for h in range(2):
            for c in range(col_tiles):
                box = (slice(8 * h, 8 * h + 8), slice(128 * c, 128 * c + 128))
                q = (g * 2 + h) * col_tiles + c
                pieces[q, 0] = factor[box]
                pieces[q, 1] = offset[box]

    pl.semaphore_wait(barrier, jnp.where(is_owner, n_owner - 1, n_owner) + n_tr - 1)

    def send_map(k, _):
        piece = lax.rem(me_ax + k, n_owner)
        to = owner_of(piece)

        @pl.when(to != me_ax)
        def _():
            pltpu.make_async_remote_copy(
                src_ref=pieces.at[piece],
                dst_ref=maps.at[me_ax],
                send_sem=send_sem.at[0],
                recv_sem=recv_sem.at[0],
                device_id=(to, me_tr),
                device_id_type=MESH,
            ).start()

        return 0

    lax.fori_loop(0, n_owner, send_map, 0)

    to_last, to_first = across.fade_up(0), across.fade_down(0)

    def prepare(g, _):
        for c in range(col_tiles):
            lanes = pl.ds(128 * c, 128)
            values = []
            for j in range(half):
                p = g * half + j
                s = solid[p, :, lanes]
                r = COUPLE * rate[p, :, lanes].astype(F32)
                driven[p, :, lanes] = r * cumul[p, :, lanes]
                values.append(s + r * (particular[p, :, lanes] - s))
                still[p, :, lanes] = values[-1]
            own[g, 0, :, lanes] = row_sums([v * to_last for v in values])
            own[g, 1, :, lanes] = row_sums([v * to_first for v in values])
        return 0

    lax.fori_loop(0, 2, prepare, 0)

    def wait_for(ref, count, sem):
        box = ref.at[pl.ds(0, count)]
        pltpu.make_async_copy(box, box, sem).wait()

    def tile_of(ref, piece):
        return ref.at[
            pl.ds(pl.multiple_of(piece // col_tiles * 8, 8), 8),
            pl.ds(pl.multiple_of(lax.rem(piece, col_tiles) * 128, 128), 128),
        ]

    @pl.when(is_owner)
    def _():
        maps[me_ax] = pieces[my_piece]
        wait_for(maps, n_ax - 1, recv_sem.at[0])

        def march(k, state):
            flows[k] = state
            return maps[k, 0] * state + maps[k, 1]

        lax.fori_loop(0, n_ax, march, tile_of(inlet, my_piece)[...], unroll=True)

        def send_flow(k, _):
            to = lax.rem(k, 4) * 8 + k // 4

            @pl.when(to != me_ax)
            def _():
                pltpu.make_async_remote_copy(
                    src_ref=flows.at[to],
                    dst_ref=tile_of(inflow, my_piece),
                    send_sem=send_sem.at[1],
                    recv_sem=recv_sem.at[1],
                    device_id=(to, me_tr),
                    device_id_type=MESH,
                ).start()

            return 0

        lax.fori_loop(0, n_ax, send_flow, 0)
        tile_of(inflow, my_piece)[...] = flows[me_ax]
        wait_for(flows, n_owner - 1, recv_sem.at[1])

    @pl.when(jnp.logical_not(is_owner))
    def _():
        wait_for(flows, n_owner, recv_sem.at[1])

    def send_sum(to):
        pltpu.make_async_remote_copy(
            src_ref=sums.at[lax.rem(to, 2), (to < me_tr).astype(jnp.int32)],
            dst_ref=sums_in.at[me_tr],
            send_sem=send_sem.at[2],
            recv_sem=recv_sem.at[2],
            device_id=(me_ax, to),
            device_id_type=MESH,
        ).start()

    def add_inflow(g, _):
        for c in range(col_tiles):
            lanes = pl.ds(128 * c, 128)
            flow = inflow[:, lanes]
            down, up = flow * to_last, flow * to_first
            values = [driven[g * half + j, :, lanes] for j in range(half)]
            last = own[g, 0, :, lanes] + row_sums([v * down for v in values])
            start = own[g, 1, :, lanes] + row_sums([v * up for v in values])
            own[g, 0, :, lanes], own[g, 1, :, lanes] = last, start
            sums[g, 0, :, lanes], sums[g, 1, :, lanes] = across.sums(me_tr, last, start)
        return 0

    lax.fori_loop(0, 2, add_inflow, 0)

    def send(to, _):
        @pl.when(to != me_tr)
        def _():
            send_sum(to)

        return 0

    lax.fori_loop(0, n_tr, send, 0)
    sums_in[me_tr] = sums[core, core]

    def finish_plane(p, _):
        gas[p] = particular[p] + cumul[p] * inflow[...]
        at = pl.ds(pl.multiple_of(p * rows, rows), rows)
        right_hi[at, :], right_lo[at, :] = split(still[p] + driven[p] * inflow[...])
        return 0

    lax.fori_loop(0, planes, finish_plane, 0, unroll=2)

    loads[5].wait()
    loads[6].wait()
    group = local.shape[1]

    def own_solve(g, _):
        at = pl.ds(pl.multiple_of(g * group, group), group)
        mid = dot3(local[0], local[1], right_hi[at, :], right_lo[at, :])
        mid_hi[at, :], mid_lo[at, :] = split(mid)
        part[at, :] = dot3(mid_hi[at, :], mid_lo[at, :], along[0], along[1])
        return 0

    lax.fori_loop(0, planes * rows // group, own_solve, 0)

    wait_for(sums_in, n_tr - 1, recv_sem.at[2])

    nothing = jnp.zeros((half, cols), F32)

    def add(k, totals):
        value = sums_in[k]
        return tuple(
            total + jnp.where(test, value, 0.0)
            for total, test in zip(totals, (k < me_tr, k > me_tr, k < twin, k > twin))
        )

    mine = lax.fori_loop(0, n_tr, add, (nothing,) * 4, unroll=True)
    twin_out[0], twin_out[1] = mine[2], mine[3]
    to_twin = pltpu.make_async_remote_copy(
        src_ref=twin_out,
        dst_ref=pairs.at[core],
        send_sem=send_sem.at[3],
        recv_sem=recv_sem.at[3],
        device_id=(me_ax, twin),
        device_id_type=MESH,
    )
    to_twin.start()
    pairs[core, 0], pairs[core, 1] = mine[0], mine[1]

    def carry_of(g):
        at = pl.ds(pl.multiple_of(g * planes, planes), planes)
        fields = across.fields(me_tr, pairs[g, 0], pairs[g, 1], own[g, 0], own[g, 1])
        end_hi, end_lo = split(jnp.concatenate(fields, axis=0))
        carry[at, :] = dot3(end_hi, end_lo, along[0], along[1])

    carry_of(core)
    to_twin.wait_recv()
    carry_of(1 - core)

    to_twin.wait_send()
    wait_for(sums_in, n_tr - 1, send_sem.at[2])

    @pl.when(is_owner)
    def _():
        wait_for(pieces, n_owner - 1, send_sem.at[0])
        wait_for(flows, n_ax - 1, send_sem.at[1])

    @pl.when(jnp.logical_not(is_owner))
    def _():
        wait_for(pieces, n_owner, send_sem.at[0])


def finish_kernel(across, gas, part, carry, gas_hbm, solid_hbm, gap_hbm, solid, gap, store_sem):
    planes, rows, cols = gas.shape
    half = planes // 2
    gas_store = pltpu.make_async_copy(gas, gas_hbm, store_sem.at[0, 0])
    gas_store.start()
    before = jnp.concatenate([across.fade_down(1)] * (cols // 128), axis=1)
    after = jnp.concatenate([across.fade_up(1)] * (cols // 128), axis=1)
    stores = []
    for p in range(planes):
        row = p // half * planes + p % half
        new = part[p] + (
            before * jnp.broadcast_to(carry[row : row + 1, :], (rows, cols))
            + after * jnp.broadcast_to(carry[row + half : row + half + 1, :], (rows, cols))
        )
        solid[p] = new
        gap[p] = gas[p] - new
        if p % 2 == 1:
            for i, (source, target) in enumerate(((solid, solid_hbm), (gap, gap_hbm))):
                box = pl.ds(p - 1, 2)
                stores.append(
                    pltpu.make_async_copy(
                        source.at[box], target.at[box], store_sem.at[1 + i, p // 2]
                    )
                )
                stores[-1].start()
    gas_store.wait()
    for store in stores:
        store.wait()


def far(value):
    return pltpu.with_memory_space_constraint(value, pltpu.HBM)


def per_device(n_ax, n_tr, solid_old, gas_rate, gas_inlet):
    planes, rows, cols = solid_old.shape
    across = Across(rows, n_tr, ACROSS_ROWS, 8)
    along = halves(line_inverse(cols, ALONG_ROW).T)
    cells = planes * rows
    half = planes // 2
    pieces = (rows // 8) * (cols // 128)
    field = (planes, rows, cols)
    anywhere = pl.BlockSpec(memory_space=pl.ANY)
    near = pl.BlockSpec(memory_space=pltpu.VMEM)
    gas, part, carry = pl.pallas_call(
        functools.partial(exchange_kernel, n_ax, n_tr, across),
        out_shape=(
            pltpu.VMEM(field, F32),
            pltpu.VMEM((cells, cols), F32),
            pltpu.VMEM((2 * planes, cols), F32),
        ),
        in_specs=[anywhere] * 5,
        out_specs=[near] * 3,
        scratch_shapes=[
            pltpu.VMEM(field, F32),
            pltpu.VMEM(field, BF16),
            pltpu.VMEM((rows, cols), F32),
            pltpu.VMEM((2, cols, cols), BF16),
            pltpu.VMEM(across.local.shape, BF16),
            pltpu.VMEM(field, F32),
            pltpu.VMEM(field, F32),
            pltpu.VMEM(field, F32),
            pltpu.VMEM(field, F32),
            pltpu.VMEM((cells, cols), BF16),
            pltpu.VMEM((cells, cols), BF16),
            pltpu.VMEM((cells, cols), BF16),
            pltpu.VMEM((cells, cols), BF16),
            pltpu.VMEM((pieces, 2, 8, 128), F32),
            pltpu.VMEM((n_ax, 2, 8, 128), F32),
            pltpu.VMEM((n_ax, 8, 128), F32),
            pltpu.VMEM((rows, cols), F32),
            pltpu.VMEM((2, 2, half, cols), F32),
            pltpu.VMEM((2, 2, half, cols), F32),
            pltpu.VMEM((n_tr, half, cols), F32),
            pltpu.VMEM((2, half, cols), F32),
            pltpu.VMEM((2, 2, half, cols), F32),
            pltpu.SemaphoreType.DMA((7,)),
            pltpu.SemaphoreType.DMA((4,)),
            pltpu.SemaphoreType.DMA((4,)),
        ],
        compiler_params=pltpu.CompilerParams(
            collective_id=0, has_side_effects=True, vmem_limit_bytes=32 * 2**20
        ),
        name="exchange",
    )(*map(far, (solid_old, gas_rate, gas_inlet, jnp.asarray(along), jnp.asarray(across.local))))

    shape = jax.ShapeDtypeStruct(field, F32)
    return pl.pallas_call(
        functools.partial(finish_kernel, across),
        out_shape=(shape, shape, shape),
        in_specs=[near] * 3,
        out_specs=[anywhere] * 3,
        scratch_shapes=[
            pltpu.VMEM(field, F32),
            pltpu.VMEM(field, F32),
            pltpu.SemaphoreType.DMA((3, planes // 2)),
        ],
        compiler_params=pltpu.CompilerParams(vmem_limit_bytes=16 * 2**20),
        name="finish",
    )(gas, part.reshape(field), carry)


def solution(mesh):
    n_ax, n_tr = mesh.shape["ax"], mesh.shape["tr"]
    return jax.shard_map(
        functools.partial(per_device, n_ax, n_tr),
        mesh=mesh,
        in_specs=(P("ax", "tr", None), P("ax", "tr", None), P("tr", None)),
        out_specs=(P("ax", "tr", None), P("ax", "tr", None), P("ax", "tr", None)),
        check_vma=False,
    )
```
